128 devices in a mesh: wide: 32 (over x, z_lo, y), narrow: 4 (over z_hi, core).
Axes of the slice: x: 4, y: 4, z: 4 (z_hi: 2, z_lo: 2; z = z_hi * 2 + z_lo), core: 2. Of those that a mesh axis runs over, the one named last changes fastest.
Arguments:
- velocity: bfloat16 [3, 512, 32, 2, 1024], P(None, 'wide', None, None, 'narrow'), may hold values from -6 to 6
- inverses: bfloat16 [8, 32, 32], replicated, may hold values from -2.4 to 2.4, as said below
- class_index: int32 [512, 1024], P('wide', 'narrow'), may hold values from 0 to 7
- keep_count: int32 [512], P('wide'), may hold values from 256 to 512, as said below
Outputs:
- advanced: float32 [3, 512, 32, 2, 1024], P(None, 'wide', None, None, 'narrow')
The draws below stay inside these ranges and needn't reach their ends.
Inputs may be any that keep to these rules, and one draw needn't show every extreme that they name: `inverses`: dense matrices standing for each wavenumber class's inverse of the implicit wall-normal operator. Mode (kx, m) of the products is kept where |m| < keep_count[kx].
All inputs are finite; a program needn't handle non-finite values.
Results may differ from the reference program's by a relative error of at most 0.0045.
Values may be sent and summed in bfloat16 or wider, within the bound.
No kernel may reach another device: no remote copies, remote signals or barrier semaphores. Data moves between devices by JAX's collectives and lax.ppermute only.
A program may use at most 64 MiB of HBM per device.

```python
import math
import jax
import jax.numpy as jnp
from jax import lax

KX = 512
KZ = 1024
NCLASS = 8
NYW = 32
PX = 1536
PZ = 1536


def draw_inverses(key, part):
    key = jax.random.fold_in(key, 11)
    key_length, key_random, key_diagonal = jax.random.split(key, 3)
    positions = jnp.arange(NYW, dtype=jnp.float32)
    distance = jnp.abs(positions[:, None] - positions[None, :])
    lengths = jnp.exp(jax.random.uniform(key_length, (NCLASS, 1, 1), jnp.float32, 0.0, math.log(max(NYW / 2.0, 1.5))))
    random_part = jnp.clip(jax.random.normal(key_random, (NCLASS, NYW, NYW), jnp.float32), -4.0, 4.0)
    coupling = 0.6 * random_part * jnp.exp(-distance / lengths)
    diagonal = 1.0 + 0.5 * jax.random.uniform(key_diagonal, (NCLASS, NYW, 1), jnp.float32)
    return jnp.where(distance == 0.0, diagonal, coupling).astype(jnp.bfloat16)


def draw_keep_count(key, part):
    key = jax.random.fold_in(key, 23)
    key_values, key_shuffle = jax.random.split(key, 2)
    values = jax.random.randint(key_values, (KX,), KZ // 4, KZ // 2 + 1, jnp.int32)
    shuffled = jax.random.permutation(key_shuffle, KX)
    values = values.at[shuffled[0]].set(KZ // 2)
    values = values.at[shuffled[1]].set(KZ // 4)
    return values.astype(jnp.int32)


def set_ends(array, own_key, smallest, top_value):
    longest = array.shape.index(max(array.shape))
    spots = []
    for shift in (0, 1):
        where = [jax.random.randint(jax.random.fold_in(own_key, axis), (), 0, length) for axis, length in enumerate(array.shape)]
        where[longest] = (where[longest] + shift) % array.shape[longest]
        spots.append(tuple(where))
    return array.at[spots[0]].set(smallest).at[spots[1]].set(top_value)


def levels(rng, dims, cuts, least, top_value):
    level, own = 1.0, jax.random.fold_in(rng, 6)
    for position, blocks in cuts:
        heights = jnp.exp(jax.random.uniform(jax.random.fold_in(own, position), (blocks,), jnp.float32, least / len(cuts), top_value / len(cuts)))
        level = level * jnp.repeat(heights, dims[position] // blocks).reshape([-1 if axis == position else 1 for axis in range(len(dims))])
    return level


def gaussian(own_key, extent, width, bound, cuts=(), kind=jnp.bfloat16):
    loudness = levels(own_key, extent, cuts, -0.22, 0.18) if cuts else 1.0
    result = jax.random.normal(own_key, extent, jnp.float32) * width * loudness
    return jnp.minimum(jnp.maximum(result, -bound), bound).astype(kind)


def setup_inputs(seed: int = 0) -> dict:
    keys = jax.random.split(jax.random.key(seed), 5)
    velocity = gaussian(keys[0], (3, KX, NYW, 2, KZ), 1.0, 6.0, ((1, 32), (4, 4)))
    inverses = draw_inverses(jax.random.fold_in(keys[4], 71), 0)
    class_index = set_ends(jax.random.randint(keys[2], (KX, KZ), 0, NCLASS), jax.random.fold_in(keys[2], 1), 0, NCLASS - 1).astype(jnp.int32)
    keep_count = draw_keep_count(jax.random.fold_in(keys[4], 71), 0)
    return {"velocity": velocity, "inverses": inverses, "class_index": class_index, "keep_count": keep_count}


def z_table():
    mode_index = jnp.arange(KZ, dtype=jnp.int32)
    wavenumber = jnp.where(mode_index < KZ // 2, mode_index, mode_index - KZ)
    points = jnp.arange(PZ, dtype=jnp.int32)
    phases = wavenumber[:, None] * points[None, :] % PZ
    angles = 2.0 * math.pi / PZ * phases.astype(jnp.float32)
    cos_part = jnp.cos(angles)
    sin_part = jnp.sin(angles)
    top_half = jnp.concatenate([cos_part, sin_part], axis=1)
    low_half = jnp.concatenate([-sin_part, cos_part], axis=1)
    return jnp.concatenate([top_half, low_half], axis=0).astype(jnp.bfloat16)

def x_tables(kx_values):
    points = jnp.arange(PX, dtype=jnp.int32)
    phases = kx_values[:, None] * points[None, :] % PX
    angles = 2.0 * math.pi / PX * phases.astype(jnp.float32)
    basis = jnp.stack([jnp.cos(angles), -jnp.sin(angles)], axis=1)
    weights = jnp.where(kx_values == 0, 1.0, 2.0).astype(jnp.float32)
    return ((weights[:, None, None] * basis).astype(jnp.bfloat16), basis.astype(jnp.bfloat16))

def transform_plane(one_plane, z_basis, x_synth, x_basis):
    mode_lines = one_plane.reshape(3 * KX, 2 * KZ)
    spread = jnp.dot(mode_lines, z_basis, preferred_element_type=jnp.float32)
    spread = spread.astype(jnp.bfloat16).reshape(3, KX, 2, PZ)
    fields = jnp.einsum('ckrb,kra->cab', spread.astype(jnp.float32), x_synth.astype(jnp.float32))
    fields = fields * (0.5 / math.sqrt(KX * KZ))
    product = (fields * fields[1:2]).astype(jnp.bfloat16)
    folded = jnp.einsum('cab,kra->ckrb', product.astype(jnp.float32), x_basis.astype(jnp.float32))
    folded = (folded / PX).astype(jnp.bfloat16)
    flat_modes = folded.reshape(3 * KX, 2 * PZ)
    spectra = jnp.dot(flat_modes, z_basis.T, preferred_element_type=jnp.float32)
    spectra = spectra * (2.0 * math.sqrt(KX * KZ) / PZ)
    return spectra.astype(jnp.bfloat16).reshape(3, KX, 2, KZ)

def reference(velocity, inverses, class_index, keep_count):
    z_basis = z_table()
    x_synth, x_basis = x_tables(jnp.arange(KX, dtype=jnp.int32))
    planes = jnp.transpose(velocity, (2, 0, 1, 3, 4))
    returned = lax.map(lambda one_plane: transform_plane(one_plane, z_basis, x_synth, x_basis), planes)
    returned = jnp.transpose(returned, (1, 2, 0, 3, 4))
    mode_index = jnp.arange(KZ, dtype=jnp.int32)
    wavenumber = jnp.where(mode_index < KZ // 2, mode_index, mode_index - KZ)
    kx_index = jnp.arange(KX, dtype=jnp.int32)
    mean_mode = (kx_index[:, None] == 0) & (wavenumber[None, :] == 0)
    keep_mask = (jnp.abs(wavenumber)[None, :] < keep_count[:, None]) & jnp.logical_not(mean_mode)
    outputs = []
    for component in range(3):
        kept = jnp.where(keep_mask[:, None, None, :], returned[component].astype(jnp.float32), 0.0)
        right_side = (velocity[component].astype(jnp.float32) + 0.5 * kept).astype(jnp.bfloat16)
        solved = jnp.zeros(right_side.shape, jnp.float32)
        for block_id in range(NCLASS):
            applied = jnp.einsum('yz,kzrj->kyrj', inverses[block_id].astype(jnp.float32), right_side.astype(jnp.float32))
            solved = jnp.where((class_index == block_id)[:, None, None, :], applied, solved)
        outputs.append(solved)
    return jnp.stack(outputs)
```

```python
import functools
import math

import jax
import jax.numpy as jnp
import ml_dtypes
import numpy as np
from jax import lax
from jax.experimental import pallas as pl
from jax.experimental.pallas import tpu as pltpu
from jax.sharding import Mesh
from jax.sharding import PartitionSpec as P

KX = 512
KZ = 1024
NCLASS = 8
PX = 1536
PZ = 1536
HALF = PX // 2
NY = 32
BF = jnp.bfloat16
VMEM = 60 * 1024 * 1024
COLUMN = ("zl", "zh", "core")
PLANE = ("x", "y")
KX_ORDER = np.concatenate([np.arange(0, 16, 2), np.arange(1, 16, 2)])


def angles(wavenumbers, points, period):
    phases = (wavenumbers[:, None] * points[None, :]) % period
    scaled = np.float32(2.0 * math.pi / period) * phases.astype(np.float32)
    return scaled.astype(np.float64)


def z_table():
    index = np.arange(KZ)
    wavenumber = np.where(index < KZ // 2, index, index - KZ)
    theta = angles(wavenumber, np.arange(PZ), PZ)
    cos_part, sin_part = np.cos(theta), np.sin(theta)
    top = np.concatenate([cos_part, sin_part], axis=1)
    low = np.concatenate([-sin_part, cos_part], axis=1)
    return np.concatenate([top, low], axis=0).astype(np.float32).astype(ml_dtypes.bfloat16)


def x_tables():
    x, y, zl, i = np.meshgrid(np.arange(4), np.arange(4), np.arange(2), np.arange(8), indexing="ij")
    synth, fold = [], []
    for parity in range(2):
        kx = (x * 8 + zl * 4 + y) * 16 + 2 * i + parity
        theta = angles(kx.reshape(-1), np.arange(HALF), PX).reshape(4, 4, 2, 8, HALF)
        basis = np.stack([np.cos(theta), -np.sin(theta)], axis=2).astype(np.float32)
        weight = np.where(kx == 0, 1.0, 2.0).astype(np.float32)[:, :, None, :, :, None]
        synth.append((weight * basis).reshape(512, HALF).T)
        fold.append(basis.reshape(512, HALF))
    return (
        np.stack(synth).astype(ml_dtypes.bfloat16),
        np.stack(fold).astype(ml_dtypes.bfloat16),
    )


def pack_matrix():
    matrix = np.zeros((256, 256), np.float32)
    for t in range(2):
        for plane in range(4):
            for ri in range(2):
                for k in range(16):
                    row = ((t * 4 + plane) * 2 + ri) * 16 + k
                    matrix[row, KX_ORDER[k] * 16 + plane * 4 + t * 2 + ri] = 1.0
    return matrix.astype(ml_dtypes.bfloat16)


def dot(a, b):
    return jnp.dot(a, b, preferred_element_type=jnp.float32)


def pack_kernel(v_ref, p_ref, out_ref):
    for group in range(8):
        rows = [v_ref[c, :, group * 16 : group * 16 + 16, :].reshape(256, 128) for c in range(3)]
        moved = dot(p_ref[...], jnp.concatenate(rows, axis=1)).astype(BF)
        for c in range(3):
            part = moved[:, c * 128 : c * 128 + 128].reshape(2, 4, 2, 16, 128)
            for t in range(2):
                out_ref[group, c, :, :, :, t * 128 : t * 128 + 128] = part[t]


def synth_kernel(r_ref, table_ref, out_ref, lhs):
    @pl.when((pl.program_id(0) == 0) & (pl.program_id(1) == 0))
    def _():
        for zl in range(2):
            for quarter in range(4):
                for ri in range(2):
                    part = r_ref[zl * 4 + quarter, :, :, ri].reshape(192, 256)
                    lhs[zl * 192 : zl * 192 + 192, pl.ds(ri * KZ + quarter * 256, 256)] = part

    lines = dot(lhs[...], table_ref[...])
    for half in range(2):
        part = lines[:, half * 384 : half * 384 + 384].reshape(2, 3, 4, 2, 8, 384)
        for plane in range(4):
            for c in range(3):
                piece = part[:, c, plane]
                mixed = jnp.concatenate([piece[zl, parity] for parity in range(2) for zl in range(2)], axis=0)
                out_ref[plane, half, c, 0] = mixed.astype(BF)


def middle_kernel(d_ref, synth_ref, fold_ref, out_ref, prod, *, scale):
    block = 256
    for step in range(HALF // block):
        rows = slice(step * block, step * block + block)
        fields = []
        for c in range(3):
            even = dot(synth_ref[0, rows, :], d_ref[:, c, :, 0:16, :].reshape(512, 384))
            odd = dot(synth_ref[1, rows, :], d_ref[:, c, :, 16:32, :].reshape(512, 384))
            fields.append((even + odd, even - odd))
        for c in range(3):
            low = fields[c][0] * fields[1][0]
            high = fields[c][1] * fields[1][1]
            prod[c, 0, rows, :] = (low + high).astype(BF)
            prod[c, 1, rows, :] = (low - high).astype(BF)
    for c in range(3):
        for parity in range(2):
            spectra = dot(fold_ref[parity], prod[c, parity]) * scale
            out_ref[:, c, :, parity * 16 : parity * 16 + 16, :] = spectra.astype(BF).reshape(16, 2, 16, 384)


def analyse_kernel(b_ref, table_ref, out_ref, lhs, *, scale):
    @pl.when((pl.program_id(0) == 0) & (pl.program_id(1) == 0))
    def _():
        for plane in range(4):
            for quarter in range(4):
                for ri in range(2):
                    part = b_ref[plane * 4 + quarter, :, ri].reshape(96, 384)
                    lhs[plane * 96 : plane * 96 + 96, pl.ds(ri * PZ + quarter * 384, 384)] = part

    spectra = scale * lax.dot_general(
        lhs[...], table_ref[...], (((1,), (1,)), ((), ())), preferred_element_type=jnp.float32
    )
    part = spectra.reshape(4, 3, 2, 2, 8, 512)
    for core in range(2):
        for zl in range(2):
            for c in range(3):
                for plane in range(4):
                    piece = part[plane, c, :, zl, :, core * 256 : core * 256 + 256]
                    out_ref[zl, 0, core, c, plane, 0] = piece.reshape(16, 256).astype(BF)


def solve_kernel(n_ref, v_ref, p_ref, w_ref, class_ref, keep_ref, out_ref, right):
    for group in range(8):
        rows = []
        for c in range(3):
            both = [
                n_ref[group, c, :, :, :, t * 128 : t * 128 + 128].reshape(128, 128) for t in range(2)
            ]
            rows.append(jnp.concatenate(both, axis=0))
        moved = dot(p_ref[...], jnp.concatenate(rows, axis=1))
        for c in range(3):
            part = moved[:, c * 128 : c * 128 + 128].reshape(16, 16, 128)
            keep = keep_ref[...]
            kept = part * jnp.concatenate([keep, keep], axis=1)
            old = v_ref[c, :, group * 16 : group * 16 + 16, :].astype(jnp.float32)
            right[:, group * 16 : group * 16 + 16, c * 128 : c * 128 + 128] = (old + kept).astype(BF)

    def one(k, _):
        applied = dot(w_ref[...], right[k]).reshape(NCLASS, 16, 8, 384)
        classes = class_ref[k]
        classes = jnp.concatenate([classes] * 3, axis=1)
        total = applied[0]
        for index in range(1, NCLASS):
            total = jnp.where((classes == index)[None], applied[index], total)
        for c in range(3):
            out_ref[c, k] = total[:, :, c * 128 : c * 128 + 128].reshape(128, 128)
        return 0

    lax.fori_loop(0, 16, one, 0)


def params():
    return pltpu.CompilerParams(vmem_limit_bytes=VMEM)


def body(velocity, inverses, class_index, keep_count):
    scale_x = (0.5 / math.sqrt(KX * KZ)) ** 2 / PX
    scale_z = 2.0 * math.sqrt(KX * KZ) / PZ
    z_basis = jnp.asarray(z_table())
    x_synth, x_fold = (jnp.asarray(t) for t in x_tables())
    mover = pack_matrix()
    lines = velocity.reshape(3, 16, NY, 2, 2, 128).transpose(0, 1, 2, 4, 3, 5).reshape(3, 16, 128, 128)
    packed = pl.pallas_call(
        pack_kernel,
        out_shape=jax.ShapeDtypeStruct((8, 3, 4, 2, 16, 256), BF),
        compiler_params=params(),
        name="pack",
    )(lines, jnp.asarray(mover))
    column = lax.all_to_all(packed, COLUMN, split_axis=0, concat_axis=0, tiled=True)
    spread = pl.pallas_call(
        synth_kernel,
        grid=(2, 2),
        in_specs=[
            pl.BlockSpec((8, 3, 4, 2, 16, 256), lambda r, q: (0,) * 6),
            pl.BlockSpec((2 * KZ, 768), lambda r, q: (0, r * 2 + q)),
        ],
        out_specs=pl.BlockSpec((4, 2, 3, 1, 32, 384), lambda r, q: (0, q, 0, r, 0, 0)),
        out_shape=jax.ShapeDtypeStruct((4, 4, 3, 2, 32, 384), BF),
        scratch_shapes=[pltpu.VMEM((384, 2 * KZ), BF)],
        compiler_params=params(),
        name="synth",
    )(column, z_basis)
    planes = lax.all_to_all(spread.reshape(16, 3, 2, 32, 384), PLANE, split_axis=0, concat_axis=0, tiled=True)
    folded = pl.pallas_call(
        functools.partial(middle_kernel, scale=scale_x),
        out_shape=jax.ShapeDtypeStruct((16, 3, 2, 32, 384), BF),
        scratch_shapes=[pltpu.VMEM((3, 2, HALF, 384), BF)],
        compiler_params=params(),
        name="middle",
    )(planes, x_synth, x_fold)
    pieces = lax.all_to_all(folded, PLANE, split_axis=0, concat_axis=0, tiled=True)
    nonlinear = pl.pallas_call(
        functools.partial(analyse_kernel, scale=scale_z),
        grid=(2, 2),
        in_specs=[
            pl.BlockSpec((16, 3, 2, 32, 384), lambda r, h: (0,) * 5),
            pl.BlockSpec((512, 2 * PZ), lambda r, h: (r * 2 + h, 0)),
        ],
        out_specs=pl.BlockSpec((2, 1, 2, 3, 4, 1, 16, 256), lambda r, h: (0, h, 0, 0, 0, r, 0, 0)),
        out_shape=jax.ShapeDtypeStruct((2, 2, 2, 3, 4, 2, 16, 256), BF),
        scratch_shapes=[pltpu.VMEM((384, 2 * PZ), BF)],
        compiler_params=params(),
        name="analyse",
    )(pieces, z_basis)
    returned = lax.all_to_all(
        nonlinear.reshape(8, 3, 4, 2, 16, 256), COLUMN, split_axis=0, concat_axis=0, tiled=True
    )

    kz_here = (lax.axis_index("zh") * 2 + lax.axis_index("core")) * 256 + jnp.arange(256, dtype=jnp.int32)
    wavenumber = jnp.where(kz_here < KZ // 2, kz_here, kz_here - KZ)
    wide = lax.axis_index("x") * 8 + lax.axis_index("zl") * 4 + lax.axis_index("y")
    kx_here = wide * 16 + jnp.arange(16, dtype=jnp.int32)
    mean_mode = (kx_here[:, None] == 0) & (wavenumber[None, :] == 0)
    keep_mask = (jnp.abs(wavenumber)[None, :] < keep_count[:, None]) & jnp.logical_not(mean_mode)

    def by_row(values):
        halves = values.reshape(16, 1, 2, 1, 128)
        return jnp.broadcast_to(halves, (16, 2, 2, 2, 128)).reshape(16, 8, 128)

    keep = by_row(jnp.where(keep_mask, 0.5, 0.0).astype(jnp.float32))
    classes = by_row(class_index)
    operators = jnp.einsum("nyz,ab->nyazb", inverses, jnp.eye(4, dtype=BF))
    operators = operators.reshape(NCLASS * 128, 128)
    solved = pl.pallas_call(
        solve_kernel,
        out_shape=jax.ShapeDtypeStruct((3, 16, 128, 128), jnp.float32),
        scratch_shapes=[pltpu.VMEM((16, 128, 384), BF)],
        compiler_params=params(),
        name="solve",
    )(returned, lines, jnp.asarray(mover.T), operators, classes, keep)
    return solved.reshape(3, 16, NY, 2, 2, 128).transpose(0, 1, 2, 4, 3, 5).reshape(3, 16, NY, 2, 256)


def solution(mesh):
    fine = Mesh(mesh.devices.reshape(4, 2, 4, 2, 2), ("x", "zl", "y", "zh", "core"))
    wide, narrow = ("x", "zl", "y"), ("zh", "core")
    in_specs = (P(None, wide, None, None, narrow), P(), P(wide, narrow), P(wide))
    out_specs = P(None, wide, None, None, narrow)
    return jax.shard_map(body, mesh=fine, in_specs=in_specs, out_specs=out_specs, check_vma=False)
```

```python
import functools
import math

import jax
import jax.numpy as jnp
import ml_dtypes
import numpy as np
from jax import lax
from jax.experimental import pallas as pl
from jax.experimental.pallas import tpu as pltpu
from jax.sharding import Mesh
from jax.sharding import PartitionSpec as P

KX = 512
KZ = 1024
NCLASS = 8
PX = 1536
PZ = 1536
HALF = PX // 2
NY = 32
BF = jnp.bfloat16
VMEM = 28 * 1024 * 1024
COLUMN = ("zl", "zh")
ORDER = (1, 0, 2)

def angles(wavenumbers, points, period):
    phases = (wavenumbers[:, None] * points[None, :]) % period
    scaled = np.float32(2.0 * math.pi / period) * phases.astype(np.float32)
    return scaled.astype(np.float64)


def z_tables():
    tables = []
    for parity in range(2):
        index = np.arange(parity, KZ, 2)
        wavenumber = np.where(index < KZ // 2, index, index - KZ)
        theta = angles(wavenumber, np.arange(HALF), PZ)
        tables.append(np.stack([np.cos(theta), np.sin(theta)]))
    return np.stack(tables).astype(np.float32).astype(ml_dtypes.bfloat16)


def x_tables():
    x, y, zl, i = np.meshgrid(np.arange(4), np.arange(4), np.arange(2), np.arange(8), indexing="ij")
    synth, fold = [], []
    for parity in range(2):
        kx = (x * 8 + zl * 4 + y) * 16 + 2 * i + parity
        theta = angles(kx.reshape(-1), np.arange(HALF), PX).reshape(4, 4, 2, 8, HALF)
        basis = np.stack([np.cos(theta), -np.sin(theta)], axis=2).astype(np.float32)
        weight = np.where(kx == 0, 1.0, 2.0).astype(np.float32)[:, :, None, :, :, None]
        synth.append((weight * basis).reshape(512, HALF).T)
        fold.append(basis.reshape(512, HALF))
    return (
        np.stack(synth).astype(ml_dtypes.bfloat16),
        np.stack(fold).astype(ml_dtypes.bfloat16),
    )


def mover(turned):
    row, column = (lax.broadcasted_iota(jnp.int32, (256, 256), axis) for axis in (turned, 1 - turned))
    kx = ((row & 7) << 1) | ((row >> 3) & 1)
    source = (kx << 4) | (((row >> 5) & 3) << 2) | ((row >> 7) << 1) | ((row >> 4) & 1)
    return (column == source).astype(jnp.float32).astype(BF)


def sorter(turned):
    row, column = (lax.broadcasted_iota(jnp.int32, (256, 256), axis) for axis in (turned, 1 - turned))
    return (row == (((column & 127) << 1) | (column >> 7))).astype(jnp.float32).astype(BF)


def wait(copies):
    for copy in copies:
        copy.wait()


def dot(a, b):
    return jnp.dot(a, b, preferred_element_type=jnp.float32)


def place_kernel(inv_ref, w_ref):
    row, column = (lax.broadcasted_iota(jnp.int32, (128, 128), axis) for axis in range(2))
    same = row % 4 == column % 4
    tall = (row[:, :32] // 4 == column[:, :32]).astype(BF)
    wide = (lax.broadcasted_iota(jnp.int32, (32, 128), 0) == lax.broadcasted_iota(jnp.int32, (32, 128), 1) // 4).astype(BF)
    for index in range(NCLASS):
        rows = dot(tall, inv_ref[index]).astype(BF)
        w_ref[:, index * 128 : index * 128 + 128] = jnp.where(same, dot(rows, wide), 0.0).astype(BF)


def cut_kernel(pos, v_hbm, o0, o1, o2, sems):
    copies = []
    for c, out in enumerate((o0, o1, o2)):
        for z in range(4):
            first = pl.multiple_of(z * 32 + (1 - pos[3]) * 16, 16)
            copies.append(pltpu.make_async_copy(v_hbm.at[c, :, pl.ds(first, 16)], out.at[z], sems.at[c, z]))
            copies[-1].start()
    wait(copies)


def pack_kernel(pos, v_hbm, *refs, parts, preload):
    nc = len(parts)
    other_refs, refs = refs[:nc], refs[nc:]
    if preload:
        table_hbm, refs = refs[0], refs[1:]
    outs, refs = refs[:4], refs[4:]
    if preload:
        table_ref, refs = refs[0], refs[1:]
    v_ref, sems = refs
    copies = []
    for i, c in enumerate(parts):
        for z in range(4):
            first = pl.multiple_of(z * 32 + pos[3] * 16, 16)
            copies.append(pltpu.make_async_copy(v_hbm.at[c, :, pl.ds(first, 16)], v_ref.at[i, z], sems.at[4 * i + z]))
            copies[-1].start()
    if preload:
        table_copy = pltpu.make_async_copy(table_hbm, table_ref, sems.at[4 * nc])
        table_copy.start()
    move, sort = mover(0), sorter(0)
    wait(copies)
    places = [(step, core) for step in range(4) for core in range(2)]
    parts = []
    for step, core in places:
        z = lax.rem(pos[2] + step, 4)
        parts += [(other_refs[i] if core else v_ref.at[i])[z].reshape(256, 128) for i in range(nc)]
    moved = dot(move, jnp.concatenate(parts, axis=1)).astype(BF)
    parts = []
    for i in range(8 * nc):
        part = moved[:, i * 128 : i * 128 + 128]
        parts.append(jnp.concatenate([part[:128], part[128:]], axis=1))
    moved = dot(jnp.concatenate(parts, axis=0), sort).astype(BF)
    for i, (step, core) in enumerate(places):
        outs[step][core] = moved[i * nc * 128 : (i + 1) * nc * 128].reshape(nc, 4, 2, 16, 256)
    if preload:
        table_copy.wait()


def gather_kernel(b0, b1, b2, b3, *rest):
    out_ref = rest[-1]
    for step, block in enumerate((b0, b1, b2, b3)):
        out_ref[step] = block[1]


def z_copies(table_hbm, table_ref, sems):
    return [pltpu.make_async_copy(table_hbm.at[p], table_ref.at[p], sems.at[p]) for p in range(2)]


def synth_kernel(pos, r0, r1, r2, r3, table, out_ref, lhs, *rest, nc):
    table_ref = table
    if rest:
        table_ref, sems = rest
        copies = z_copies(table, table_ref, sems)
        for copy in copies:
            copy.start()
    for step, block in enumerate((r0, r1, r2, r3)):
        z = lax.rem(pos[2] + 4 - step, 4)
        for core in range(2):
            quarter = (z // 2) * 2 + lax.rem(pos[3] + core, 2)
            lanes = pl.ds(pl.multiple_of(quarter * 128, 128), 128)
            for ri in range(2):
                rows = pl.ds(pl.multiple_of(ri * (128 * nc) + lax.rem(z, 2) * (64 * nc), 64), 64 * nc)
                part = block[core, :, :, ri].reshape(64 * nc, 256)
                for parity in range(2):
                    lhs[parity, rows, lanes] = part[:, parity * 128 : parity * 128 + 128]
    if rest:
        wait(copies)
    n = 128 * nc
    sums = []
    for parity in range(2):
        by_cos = dot(lhs[parity], table_ref[parity, 0])
        by_sin = dot(lhs[parity], table_ref[parity, 1])
        sums.append((by_cos[:n] - by_sin[n:], by_sin[:n] + by_cos[n:]))
    for ri in range(2):
        even, odd = sums[0][ri], sums[1][ri]
        for half, both in enumerate((even + odd, even - odd)):
            part = both.reshape(2, nc, 4, 2, 8, HALF)
            for plane in range(4):
                for c in range(nc):
                    mixed = [part[zl, c, plane, parity] for parity in range(2) for zl in range(2)]
                    mixed = jnp.concatenate(mixed, axis=0).astype(BF)
                    for quarter in range(2):
                        out_ref[plane * 4 + half * 2 + quarter, c, ri] = mixed[:, quarter * 384 : quarter * 384 + 384]


def middle_kernel(d_ref, *rest, scale, nc, first):
    if first:
        synth_hbm, fold_hbm, *outs, wall_ref, data, prod, synth_ref, fold_ref, sems = rest
    else:
        wall_ref, synth_hbm, fold_hbm, *outs, data, prod, synth_ref, fold_ref, sems = rest
    synth_copy = pltpu.make_async_copy(synth_hbm, synth_ref, sems.at[0])
    fold_copy = pltpu.make_async_copy(fold_hbm, fold_ref, sems.at[1])
    synth_copy.start()
    for parity in range(2):
        for c in range(nc):
            part = d_ref[:, c, :, parity * 16 : parity * 16 + 16, :].reshape(512, 384)
            data[parity, :, c * 384 : c * 384 + 384] = part
    synth_copy.wait()
    fold_copy.start()
    for step in range(3):
        rows = slice(step * 256, step * 256 + 256)
        even = dot(synth_ref[0, rows, :], data[0])
        odd = dot(synth_ref[1, rows, :], data[1])
        low, high = even + odd, even - odd
        if first:
            wall_ref[0, rows, :] = low
            wall_ref[1, rows, :] = high
        for c in range(nc):
            lanes = slice(c * 384, c * 384 + 384)
            if first:
                one, two = low * low, high * high
            else:
                one, two = low[:, lanes] * wall_ref[0, rows, :], high[:, lanes] * wall_ref[1, rows, :]
            prod[0, rows, lanes] = (one + two).astype(BF)
            prod[1, rows, lanes] = (one - two).astype(BF)
    fold_copy.wait()
    for parity in range(2):
        spectra = (dot(fold_ref[parity], prod[parity]) * scale).astype(BF)
        for c in range(nc):
            part = spectra[:, c * 384 : c * 384 + 384].reshape(16, 2, 16, 384)
            outs[c][:, 0, :, parity * 16 : parity * 16 + 16, :] = part


def analyse_kernel(pos, b_ref, table_hbm, o0, o1, o2, o3, lhs, modes, table_ref, sems, *, scale, nc):
    copies = z_copies(table_hbm, table_ref, sems)
    for copy in copies:
        copy.start()
    n = 128 * nc
    for plane in range(4):
        for quarter in range(2):
            for ri in range(2):
                low = b_ref[plane * 4 + quarter, :, ri].reshape(32 * nc, 384).astype(jnp.float32)
                high = b_ref[plane * 4 + quarter + 2, :, ri].reshape(32 * nc, 384).astype(jnp.float32)
                rows = slice(ri * n + plane * 32 * nc, ri * n + plane * 32 * nc + 32 * nc)
                lanes = slice(quarter * 384, quarter * 384 + 384)
                lhs[0, rows, lanes] = (low + high).astype(BF)
                lhs[1, rows, lanes] = (low - high).astype(BF)
    for parity in range(2):
        copies[parity].wait()
        by_cos, by_sin = (
            lax.dot_general(
                lhs[parity], table_ref[parity, i], (((1,), (1,)), ((), ())), preferred_element_type=jnp.float32
            )
            for i in range(2)
        )
        for ri, spectra in enumerate((by_cos[:n] + by_sin[n:], by_cos[n:] - by_sin[:n])):
            part = (spectra * scale).reshape(4, nc, 2, 2, 8, 512)
            for zl in range(2):
                for quarter in range(4):
                    for plane in range(4):
                        for c in range(nc):
                            piece = part[plane, c, :, zl, :, quarter * 128 : quarter * 128 + 128]
                            block = (quarter // 2) * 2 + zl
                            lanes = slice(parity * 128, parity * 128 + 128)
                            modes[block, quarter % 2, c, plane, ri, :, lanes] = piece.reshape(16, 128).astype(BF)
    for step, out in enumerate((o0, o1, o2, o3)):
        for other in range(2):
            out[other] = modes[lax.rem(pos[2] + step, 4), lax.rem(pos[3] + other, 2)]


def solve_kernel(pos, count_ref, n0, n1, n2, n3, other_ref, v_ref, w_ref, class_ref, *rest, c, place):
    out_ref, right, done, sems = rest[-4:]
    move, sort = mover(1), sorter(1)
    row = lax.broadcasted_iota(jnp.int32, (16, 16, 128), 1)
    kx = lax.broadcasted_iota(jnp.int32, (16, 16, 128), 0)
    lane = lax.broadcasted_iota(jnp.int32, (16, 16, 128), 2)
    index = ((pos[2] // 2) * 2 + pos[3]) * 256 + lane + 128 * (lax.rem(row, 4) // 2)
    wavenumber = jnp.where(index < KZ // 2, index, index - KZ)
    counts = jnp.concatenate([jnp.full((1, 16, 128), count_ref[k], jnp.int32) for k in range(16)], axis=0)
    mean = (kx + pos[4] == 0) & (wavenumber == 0)
    half = jnp.where((jnp.abs(wavenumber) < counts) & jnp.logical_not(mean), 0.5, 0.0).astype(jnp.float32)
    own = (n0, n1, n2, n3)
    places = [(step, other) for step in range(4) for other in range(2)]
    parts = [other_ref[step, place] if other else own[step][0, place] for step, other in places]
    both = dot(jnp.concatenate([part.reshape(128, 256) for part in parts], axis=0), sort).astype(BF)
    both = [both[i * 128 : i * 128 + 128] for i in range(8)]
    both = [jnp.concatenate([part[:, :128], part[:, 128:]], axis=0) for part in both]
    moved = dot(move, jnp.concatenate(both, axis=1))
    for i, (step, other) in enumerate(places):
        group = lax.rem(pos[2] + 4 - step, 4) * 2 + lax.rem(pos[3] + other, 2)
        rows = pl.ds(pl.multiple_of(group * 16, 16), 16)
        old = v_ref[c, :, rows, :].astype(jnp.float32)
        new = (old + moved[:, i * 128 : i * 128 + 128].reshape(16, 16, 128) * half).astype(BF)
        for k in range(16):
            right[k // 2, rows, (k % 2) * 128 : (k % 2) * 128 + 128] = new[k]

    early = (lax.broadcasted_iota(jnp.int32, (16, 128), 0) & 3) < 2
    copies = []
    for pair in range(8):
        classes = []
        for k in range(2):
            line = class_ref[pair * 2 + k : pair * 2 + k + 1, :]
            classes.append(jnp.where(early, line[:, :128], line[:, 128:]))
        classes = jnp.concatenate(classes, axis=1)
        line = right[pair].reshape(8, 16, 256)
        masked = []
        for index in range(NCLASS):
            chosen = (classes == index).astype(jnp.float32).astype(BF)
            masked.append((line * chosen[None]).reshape(128, 256))
        total = dot(w_ref[...], jnp.concatenate(masked, axis=0))
        for k in range(2):
            done[pair * 2 + k] = total[:, k * 128 : k * 128 + 128]
        block = pl.ds(pair * 2, 2)
        copies.append(pltpu.make_async_copy(done.at[block], out_ref.at[c, block], sems.at[pair]))
        copies[-1].start()
    wait(copies)


MICROSECONDS = {
    "cut": 1, "place": 1, "gather": 1, "pack": 3, "solve": 3,
    "synth_first": 3, "synth_second": 40, "middle": 4, "analyse": 4,
}


def cost(name):
    return pl.CostEstimate(flops=MICROSECONDS[name] * 10**9, bytes_accessed=2**20, transcendentals=0)


def params():
    return pltpu.CompilerParams(vmem_limit_bytes=VMEM)


def in_hbm(array):
    return pltpu.with_memory_space_constraint(array, pltpu.HBM)


def spec(memory):
    return pl.BlockSpec(memory_space=memory)


def call(kernel, name, outs, args, tables, scratch, flops, scalars=1):
    specs = [spec(pltpu.SMEM)] * scalars + [spec(pltpu.VMEM)] * (len(args) - scalars) + [spec(pltpu.HBM)] * len(tables)
    return pl.pallas_call(
        kernel,
        in_specs=specs,
        out_specs=[spec(pltpu.VMEM)] * len(outs),
        out_shape=outs,
        scratch_shapes=scratch,
        compiler_params=params(),
        cost_estimate=cost(name),
        name=name,
    )(*args, *tables)


def shift(block, axes, step, size):
    places = [0, 2, 1, 3] if axes == COLUMN else range(size)
    return lax.ppermute(block, axes, [(places[j], places[(j + step) % size]) for j in range(size)])


def along_z(blocks):
    moved = {s: shift(blocks[s], COLUMN, s, 4) for s in (1, 3, 2)}
    return [blocks[0], moved[1], moved[2], moved[3]]


def across(moved, *earlier):
    shape = moved[0].shape[1:]
    other = pl.pallas_call(
        gather_kernel,
        in_specs=[spec(pltpu.VMEM)] * 4 + [spec(pl.ANY)] * len(earlier),
        out_specs=spec(pltpu.VMEM),
        out_shape=jax.ShapeDtypeStruct((4, *shape), BF),
        compiler_params=params(),
        cost_estimate=cost("gather"),
        name="gather",
    )(*moved, *earlier)
    return (*moved, shift(other, "core", 1, 2))


def plane(blocks):
    return lax.all_to_all(blocks, ("x", "y"), split_axis=0, concat_axis=0, tiled=True)


def after(value, *earlier):
    return lax.optimization_barrier((value, *earlier))[0]


def body(velocity, inverses, class_index, keep_count):
    scale_x = (0.5 / math.sqrt(KX * KZ)) ** 2 / PX
    scale_z = 2.0 * math.sqrt(KX * KZ) / PZ
    z_basis, x_synth, x_fold = (in_hbm(jnp.asarray(t)) for t in (z_tables(), *x_tables()))
    z_scratch = [pltpu.VMEM((2, 2, 512, HALF), BF), pltpu.SemaphoreType.DMA((2,))]
    lines = velocity.reshape(3, 16, NY, 2, 2, 128).transpose(0, 1, 2, 4, 3, 5).reshape(3, 16, 128, 128)
    x, y, zl = (lax.axis_index(name) for name in ("x", "y", "zl"))
    pos = jnp.stack([x, y, lax.axis_index("zh") * 2 + zl, lax.axis_index("core"), (x * 8 + zl * 4 + y) * 16])

    def mode_shape(nc):
        return jax.ShapeDtypeStruct((2, nc, 4, 2, 16, 256), BF)

    def plane_shape(nc):
        return jax.ShapeDtypeStruct((16, nc, 2, 32, 384), BF)

    table_shape = pltpu.VMEM((2, 2, 512, HALF), BF)

    def pack(parts, preload):
        nc = len(parts)
        args = [pos, in_hbm(lines), *[others[c] for c in parts]] + [z_basis] * preload
        specs = [spec(pltpu.SMEM), spec(pltpu.HBM)] + [spec(pltpu.VMEM)] * nc + [spec(pltpu.HBM)] * preload
        return pl.pallas_call(
            functools.partial(pack_kernel, parts=parts, preload=preload),
            in_specs=specs,
            out_specs=[spec(pltpu.VMEM)] * (4 + preload),
            out_shape=[mode_shape(nc)] * 4 + [table_shape] * preload,
            scratch_shapes=[pltpu.VMEM((nc, 4, 16, 16, 128), BF), pltpu.SemaphoreType.DMA((4 * nc + 1,))],
            compiler_params=params(),
            cost_estimate=cost("pack"),
            name="pack",
        )(*args)

    def synth(blocks, table):
        nc = blocks[0].shape[1]
        kernel = functools.partial(synth_kernel, nc=nc)
        scratch = [pltpu.VMEM((2, 256 * nc, 512), BF)]
        args, tables = (pos, *blocks), (z_basis,)
        if table is None:
            scratch += z_scratch
        else:
            args, tables = (pos, *blocks, table), ()
        return call(kernel, "synth_first" if table is not None else "synth_second", [plane_shape(nc)], args, tables, scratch, nc * 1.5e9)[0]

    def middle(block, wall=None):
        nc, first = block.shape[1], wall is None
        outs, args = [plane_shape(1)] * nc, (block,)
        if first:
            outs.append(jax.ShapeDtypeStruct((2, HALF, 384), jnp.float32))
        else:
            args = (block, wall)
        scratch = [pltpu.VMEM((2, 512, nc * 384), BF), pltpu.VMEM((2, HALF, nc * 384), BF)]
        scratch += [pltpu.VMEM((2, HALF, 512), BF), pltpu.VMEM((2, 512, HALF), BF), pltpu.SemaphoreType.DMA((2,))]
        kernel = functools.partial(middle_kernel, scale=scale_x, nc=nc, first=first)
        return call(kernel, "middle", outs, args, (x_synth, x_fold), scratch, 2e9, scalars=0)

    def analyse(block):
        nc = block.shape[1]
        scratch = [pltpu.VMEM((2, 256 * nc, HALF), BF), pltpu.VMEM((4, 2, nc, 4, 2, 16, 256), BF), *z_scratch]
        kernel = functools.partial(analyse_kernel, scale=scale_z, nc=nc)
        return call(kernel, "analyse", [mode_shape(nc)] * 4, (pos, block), (z_basis,), scratch, nc * 1.5e9)

    def solve(c, place, blocks, solved):
        args = [pos, keep_count, *blocks, lines, operators, class_index]
        specs = [spec(pltpu.SMEM)] * 2 + [spec(pltpu.VMEM)] * (len(args) - 2)
        aliases = {}
        if solved is not None:
            specs.append(spec(pl.ANY))
            aliases = {len(args): 0}
            args.append(solved)
        return pl.pallas_call(
            functools.partial(solve_kernel, c=c, place=place),
            in_specs=specs,
            out_specs=spec(pl.ANY),
            out_shape=jax.ShapeDtypeStruct((3, 16, 128, 128), jnp.float32),
            scratch_shapes=[
                pltpu.VMEM((8, 128, 256), BF),
                pltpu.VMEM((16, 128, 128), jnp.float32),
                pltpu.SemaphoreType.DMA((8,)),
            ],
            input_output_aliases=aliases,
            compiler_params=params(),
            cost_estimate=cost("solve"),
            name="solve",
        )(*args)

    operators = pl.pallas_call(
        place_kernel,
        out_shape=jax.ShapeDtypeStruct((128, NCLASS * 128), BF),
        compiler_params=params(),
        cost_estimate=cost("place"),
        name="place",
    )(inverses)

    one, two = (1,), (0, 2)
    pieces = pl.pallas_call(
        cut_kernel,
        in_specs=[spec(pltpu.SMEM), spec(pltpu.HBM)],
        out_specs=[spec(pltpu.VMEM)] * 3,
        out_shape=[jax.ShapeDtypeStruct((4, 16, 16, 128), BF)] * 3,
        scratch_shapes=[pltpu.SemaphoreType.DMA((3, 4))],
        compiler_params=params(),
        cost_estimate=cost("cut"),
        name="cut",
    )(pos, in_hbm(lines))
    others = {c: shift(pieces[c], "core", 1, 2) for c in (1, 0, 2)}
    packed_one = pack(one, False)
    *packed_two, table = pack(two, True)
    lines_one = synth(along_z(packed_one), table)
    lines_two = synth(along_z(packed_two), None)
    plane_one = plane(lines_one)
    plane_two = plane(after(lines_two, plane_one))
    folded_v, wall = middle(plane_one)
    folded_u, folded_w = middle(plane_two, wall)
    back_v = plane(after(folded_v, plane_two))
    back_u = plane(after(folded_u, back_v))
    modes_v = analyse(back_v)
    back_w = plane(after(folded_w, back_u, *modes_v))
    modes_u, modes_w = analyse(back_u), analyse(back_w)
    moved_v, moved_u, moved_w = (along_z(modes) for modes in (modes_v, modes_u, modes_w))
    all_v = across(moved_v, modes_u[0])
    solved = solve(1, 0, all_v, None)
    all_u = across(moved_u, modes_w[0])
    solved = solve(0, 0, all_u, solved)
    all_w = across(moved_w, all_u[4])
    solved = solve(2, 0, all_w, solved)
    return solved.reshape(3, 16, NY, 2, 2, 128).transpose(0, 1, 2, 4, 3, 5).reshape(3, 16, NY, 2, 256)


def solution(mesh):
    fine = Mesh(mesh.devices.reshape(4, 2, 4, 2, 2), ("x", "zl", "y", "zh", "core"))
    wide, narrow = ("x", "zl", "y"), ("zh", "core")
    in_specs = (P(None, wide, None, None, narrow), P(), P(wide, narrow), P(wide))
    out_specs = P(None, wide, None, None, narrow)
    return jax.shard_map(body, mesh=fine, in_specs=in_specs, out_specs=out_specs, check_vma=False)
```

```python
import functools
import math

import jax
import jax.numpy as jnp
import ml_dtypes
import numpy as np
from jax import lax
from jax.experimental import pallas as pl
from jax.experimental.pallas import tpu as pltpu
from jax.sharding import Mesh
from jax.sharding import PartitionSpec as P

KX = 512
KZ = 1024
NCLASS = 8
PX = 1536
PZ = 1536
HALF = PX // 2
NY = 32
BF = jnp.bfloat16
VMEM = 28 * 1024 * 1024
COLUMN = ("zl", "zh")
EARLY = 1
ORDER = (1, 0, 2)

def angles(wavenumbers, points, period):
    phases = (wavenumbers[:, None] * points[None, :]) % period
    scaled = np.float32(2.0 * math.pi / period) * phases.astype(np.float32)
    return scaled.astype(np.float64)


def z_tables():
    tables = []
    for parity in range(2):
        index = np.arange(parity, KZ, 2)
        wavenumber = np.where(index < KZ // 2, index, index - KZ)
        theta = angles(wavenumber, np.arange(HALF), PZ)
        tables.append(np.stack([np.cos(theta), np.sin(theta)]))
    return np.stack(tables).astype(np.float32).astype(ml_dtypes.bfloat16)


def x_tables():
    x, y, zl, i = np.meshgrid(np.arange(4), np.arange(4), np.arange(2), np.arange(8), indexing="ij")
    synth, fold = [], []
    for parity in range(2):
        kx = (x * 8 + zl * 4 + y) * 16 + 2 * i + parity
        theta = angles(kx.reshape(-1), np.arange(HALF), PX).reshape(4, 4, 2, 8, HALF)
        basis = np.stack([np.cos(theta), -np.sin(theta)], axis=2).astype(np.float32)
        weight = np.where(kx == 0, 1.0, 2.0).astype(np.float32)[:, :, None, :, :, None]
        synth.append((weight * basis).reshape(512, HALF).T)
        fold.append(basis.reshape(512, HALF))
    return (
        np.stack(synth).astype(ml_dtypes.bfloat16),
        np.stack(fold).astype(ml_dtypes.bfloat16),
    )


def mover(turned):
    row, column = (lax.broadcasted_iota(jnp.int32, (256, 256), axis) for axis in (turned, 1 - turned))
    kx = ((row & 7) << 1) | ((row >> 3) & 1)
    source = (kx << 4) | (((row >> 5) & 3) << 2) | ((row >> 7) << 1) | ((row >> 4) & 1)
    return (column == source).astype(jnp.float32).astype(BF)


def sorter(turned):
    row, column = (lax.broadcasted_iota(jnp.int32, (256, 256), axis) for axis in (turned, 1 - turned))
    return (row == (((column & 127) << 1) | (column >> 7))).astype(jnp.float32).astype(BF)


def wait(copies):
    for copy in copies:
        copy.wait()


def dot(a, b):
    return jnp.dot(a, b, preferred_element_type=jnp.float32)


def place_kernel(inv_ref, w_ref):
    row, column = (lax.broadcasted_iota(jnp.int32, (128, 128), axis) for axis in range(2))
    same = row % 4 == column % 4
    tall = (row[:, :32] // 4 == column[:, :32]).astype(BF)
    wide = (lax.broadcasted_iota(jnp.int32, (32, 128), 0) == lax.broadcasted_iota(jnp.int32, (32, 128), 1) // 4).astype(BF)
    for index in range(NCLASS):
        rows = dot(tall, inv_ref[index]).astype(BF)
        w_ref[:, index * 128 : index * 128 + 128] = jnp.where(same, dot(rows, wide), 0.0).astype(BF)


def cut_kernel(pos, v_hbm, out_ref, sems):
    copies = []
    for c in range(3):
        for z in range(4):
            first = pl.multiple_of(z * 32 + (1 - pos[3]) * 16, 16)
            copies.append(pltpu.make_async_copy(v_hbm.at[c, :, pl.ds(first, 16)], out_ref.at[c, z], sems.at[c, z]))
            copies[-1].start()
    wait(copies)


def pack_kernel(pos, v_hbm, other_ref, o0, o1, o2, o3, v_ref, sems):
    outs = (o0, o1, o2, o3)
    copies = []
    for c in range(3):
        for z in range(4):
            first = pl.multiple_of(z * 32 + pos[3] * 16, 16)
            copies.append(pltpu.make_async_copy(v_hbm.at[c, :, pl.ds(first, 16)], v_ref.at[c, z], sems.at[c, z]))
            copies[-1].start()
    move, sort = mover(0), sorter(0)
    wait(copies)
    places = [(step, core) for step in range(4) for core in range(2)]
    parts = []
    for step, core in places:
        z = lax.rem(pos[2] + step, 4)
        parts += [(other_ref if core else v_ref)[c, z].reshape(256, 128) for c in range(3)]
    moved = dot(move, jnp.concatenate(parts, axis=1)).astype(BF)
    parts = []
    for i in range(24):
        part = moved[:, i * 128 : i * 128 + 128]
        parts.append(jnp.concatenate([part[:128], part[128:]], axis=1))
    moved = dot(jnp.concatenate(parts, axis=0), sort).astype(BF)
    for i, (step, core) in enumerate(places):
        outs[step][core] = moved[i * 384 : (i + 1) * 384].reshape(3, 4, 2, 16, 256)


def hold_kernel(token, a0, a1, a2, o0, o1, o2):
    pass


def gather_kernel(n_ref, out_ref):
    out_ref[...] = n_ref[:, 1]


def z_copies(table_hbm, table_ref, sems):
    return [pltpu.make_async_copy(table_hbm.at[p], table_ref.at[p], sems.at[p]) for p in range(2)]


def synth_kernel(pos, r0, e1, e2, e3, l1, l2, l3, table_hbm, out_ref, lhs, table_ref, sems):
    nc = 3
    copies = z_copies(table_hbm, table_ref, sems)
    for copy in copies:
        copy.start()

    def fill(step, block):
        z = lax.rem(pos[2] + 4 - step, 4)
        for core in range(2):
            quarter = (z // 2) * 2 + lax.rem(pos[3] + core, 2)
            lanes = pl.ds(pl.multiple_of(quarter * 128, 128), 128)
            for ri in range(2):
                rows = pl.ds(pl.multiple_of(ri * (128 * nc) + lax.rem(z, 2) * (64 * nc), 64), 64 * nc)
                part = block[core, :, :, ri].reshape(64 * nc, 256)
                for parity in range(2):
                    lhs[parity, rows, lanes] = part[:, parity * 128 : parity * 128 + 128]

    fill(0, r0)

    @pl.when(pos[3] == EARLY)
    def _():
        for step, block in enumerate((e1, e2, e3)):
            fill(step + 1, block)

    @pl.when(pos[3] != EARLY)
    def _():
        for step, block in enumerate((l1, l2, l3)):
            fill(step + 1, block)

    n = 128 * nc
    sums = []
    for parity in range(2):
        copies[parity].wait()
        by_cos = dot(lhs[parity], table_ref[parity, 0])
        by_sin = dot(lhs[parity], table_ref[parity, 1])
        sums.append((by_cos[:n] - by_sin[n:], by_sin[:n] + by_cos[n:]))
    for ri in range(2):
        even, odd = sums[0][ri], sums[1][ri]
        for half, both in enumerate((even + odd, even - odd)):
            part = both.reshape(2, nc, 4, 2, 8, HALF)
            for plane in range(4):
                for c in range(nc):
                    mixed = [part[zl, c, plane, parity] for parity in range(2) for zl in range(2)]
                    mixed = jnp.concatenate(mixed, axis=0).astype(BF)
                    for quarter in range(2):
                        out_ref[plane * 4 + half * 2 + quarter, c, ri] = mixed[:, quarter * 384 : quarter * 384 + 384]


def middle_kernel(d_ref, synth_hbm, fold_hbm, out_ref, data, prod, synth_ref, fold_ref, sems, *, scale):
    synth_copy = pltpu.make_async_copy(synth_hbm, synth_ref, sems.at[0])
    fold_copy = pltpu.make_async_copy(fold_hbm, fold_ref, sems.at[1])
    synth_copy.start()
    for parity in range(2):
        for c in range(3):
            part = d_ref[:, c, :, parity * 16 : parity * 16 + 16, :].reshape(512, 384)
            data[parity, :, c * 384 : c * 384 + 384] = part
    synth_copy.wait()
    fold_copy.start()
    for step in range(3):
        rows = slice(step * 256, step * 256 + 256)
        even = dot(synth_ref[0, rows, :], data[0])
        odd = dot(synth_ref[1, rows, :], data[1])
        low, high = even + odd, even - odd
        for c in range(3):
            lanes = slice(c * 384, c * 384 + 384)
            one, two = low[:, lanes] * low[:, 384:768], high[:, lanes] * high[:, 384:768]
            prod[0, rows, lanes] = (one + two).astype(BF)
            prod[1, rows, lanes] = (one - two).astype(BF)
    fold_copy.wait()
    for parity in range(2):
        spectra = (dot(fold_ref[parity], prod[parity]) * scale).astype(BF)
        for c in range(3):
            part = spectra[:, c * 384 : c * 384 + 384].reshape(16, 2, 16, 384)
            out_ref[:, c, :, parity * 16 : parity * 16 + 16, :] = part


def analyse_kernel(pos, b_ref, table_hbm, out_ref, lhs, table_ref, sems, *, scale):
    nc = 3
    copies = z_copies(table_hbm, table_ref, sems)
    for copy in copies:
        copy.start()
    n = 128 * nc
    for plane in range(4):
        for quarter in range(2):
            for ri in range(2):
                low = b_ref[plane * 4 + quarter, :, ri].reshape(32 * nc, 384).astype(jnp.float32)
                high = b_ref[plane * 4 + quarter + 2, :, ri].reshape(32 * nc, 384).astype(jnp.float32)
                rows = slice(ri * n + plane * 32 * nc, ri * n + plane * 32 * nc + 32 * nc)
                lanes = slice(quarter * 384, quarter * 384 + 384)
                lhs[0, rows, lanes] = (low + high).astype(BF)
                lhs[1, rows, lanes] = (low - high).astype(BF)
    for parity in range(2):
        copies[parity].wait()
        by_cos, by_sin = (
            lax.dot_general(
                lhs[parity], table_ref[parity, i], (((1,), (1,)), ((), ())), preferred_element_type=jnp.float32
            )
            for i in range(2)
        )
        for ri, spectra in enumerate((by_cos[:n] + by_sin[n:], by_cos[n:] - by_sin[:n])):
            part = (spectra * scale).reshape(4, nc, 2, 2, 8, 512)
            for zl in range(2):
                for quarter in range(4):
                    for plane in range(4):
                        for c in range(nc):
                            piece = part[plane, c, :, zl, :, quarter * 128 : quarter * 128 + 128]
                            block, other = zl * 2 + quarter // 2, lax.rem(quarter + pos[3], 2)
                            lanes = slice(parity * 128, parity * 128 + 128)
                            out_ref[block, other, c, plane, ri, :, lanes] = piece.reshape(16, 128).astype(BF)


def solve_kernel(pos, count_ref, n_ref, other_ref, v_ref, w_ref, class_ref, out_ref, right, done, sems):
    move, sort = mover(1), sorter(1)
    row = lax.broadcasted_iota(jnp.int32, (16, 16, 128), 1)
    kx = lax.broadcasted_iota(jnp.int32, (16, 16, 128), 0)
    lane = lax.broadcasted_iota(jnp.int32, (16, 16, 128), 2)
    index = ((pos[2] // 2) * 2 + pos[3]) * 256 + lane + 128 * (lax.rem(row, 4) // 2)
    wavenumber = jnp.where(index < KZ // 2, index, index - KZ)
    counts = jnp.concatenate([jnp.full((1, 16, 128), count_ref[k], jnp.int32) for k in range(16)], axis=0)
    mean = (kx + pos[4] == 0) & (wavenumber == 0)
    half = jnp.where((jnp.abs(wavenumber) < counts) & jnp.logical_not(mean), 0.5, 0.0).astype(jnp.float32)
    places = [(block, other) for block in range(4) for other in range(2)]
    parts = [other_ref[block, c] if other else n_ref[block, 0, c] for block, other in places for c in range(3)]
    both = dot(jnp.concatenate([part.reshape(128, 256) for part in parts], axis=0), sort).astype(BF)
    both = [both[i * 128 : i * 128 + 128] for i in range(24)]
    both = [jnp.concatenate([part[:, :128], part[:, 128:]], axis=0) for part in both]
    moved = dot(move, jnp.concatenate(both, axis=1))
    for i, (block, other) in enumerate(places):
        z = (block % 2) * 2 + block // 2
        group = z * 2 + lax.rem(pos[3] + other, 2)
        rows = pl.ds(pl.multiple_of(group * 16, 16), 16)
        for c in range(3):
            old = v_ref[c, :, rows, :].astype(jnp.float32)
            lanes = slice((i * 3 + c) * 128, (i * 3 + c) * 128 + 128)
            new = (old + moved[:, lanes].reshape(16, 16, 128) * half).astype(BF)
            for k in range(16):
                right[k // 2, rows, (c * 2 + k % 2) * 128 : (c * 2 + k % 2) * 128 + 128] = new[k]

    early = (lax.broadcasted_iota(jnp.int32, (16, 128), 0) & 3) < 2
    copies = []
    for pair in range(8):
        classes = []
        for k in range(2):
            line = class_ref[pair * 2 + k : pair * 2 + k + 1, :]
            classes.append(jnp.where(early, line[:, :128], line[:, 128:]))
        classes = jnp.concatenate(classes * 3, axis=1)
        line = right[pair].reshape(8, 16, 768)
        masked = []
        for index in range(NCLASS):
            chosen = (classes == index).astype(jnp.float32).astype(BF)
            masked.append((line * chosen[None]).reshape(128, 768))
        total = dot(w_ref[...], jnp.concatenate(masked, axis=0))
        block = pl.ds(pair * 2, 2)
        for c in range(3):
            for k in range(2):
                done[c, pair * 2 + k] = total[:, (c * 2 + k) * 128 : (c * 2 + k) * 128 + 128]
            copies.append(pltpu.make_async_copy(done.at[c, block], out_ref.at[c, block], sems.at[c, pair]))
            copies[-1].start()
    wait(copies)


def params():
    return pltpu.CompilerParams(vmem_limit_bytes=VMEM)


def in_hbm(array):
    return pltpu.with_memory_space_constraint(array, pltpu.HBM)


def spec(memory):
    return pl.BlockSpec(memory_space=memory)


def along_z(block, step, core):
    pairs = []
    for z in range(4):
        to = (z + step) % 4
        pairs.append((((z % 2) * 2 + z // 2) * 2 + core, ((to % 2) * 2 + to // 2) * 2 + core))
    return lax.ppermute(block, ("zl", "zh", "core"), pairs)


def plane(blocks):
    return lax.all_to_all(blocks, ("x", "y"), split_axis=0, concat_axis=0, tiled=True)


def after(value, *earlier):
    return lax.optimization_barrier((value, *earlier))[0]


def body(velocity, inverses, class_index, keep_count):
    scale_x = (0.5 / math.sqrt(KX * KZ)) ** 2 / PX
    scale_z = 2.0 * math.sqrt(KX * KZ) / PZ
    z_basis, x_synth, x_fold = (in_hbm(jnp.asarray(t)) for t in (z_tables(), *x_tables()))
    z_scratch = [pltpu.VMEM((2, 2, 512, HALF), BF), pltpu.SemaphoreType.DMA((2,))]
    lines = velocity.reshape(3, 16, NY, 2, 2, 128).transpose(0, 1, 2, 4, 3, 5).reshape(3, 16, 128, 128)
    x, y, zl = (lax.axis_index(name) for name in ("x", "y", "zl"))
    pos = jnp.stack([x, y, lax.axis_index("zh") * 2 + zl, lax.axis_index("core"), (x * 8 + zl * 4 + y) * 16])

    mode_shape = jax.ShapeDtypeStruct((2, 3, 4, 2, 16, 256), BF)
    plane_shape = jax.ShapeDtypeStruct((16, 3, 2, 32, 384), BF)
    smem, vmem, hbm, free = (spec(m) for m in (pltpu.SMEM, pltpu.VMEM, pltpu.HBM, pl.ANY))

    def call(kernel, name, specs, args, outs, scratch, aliases={}, out_spec=vmem):
        return pl.pallas_call(
            kernel,
            in_specs=specs,
            out_specs=[out_spec] * len(outs),
            out_shape=outs,
            scratch_shapes=scratch,
            input_output_aliases=aliases,
            compiler_params=params(),
            name=name,
        )(*args)

    operators = pl.pallas_call(
        place_kernel,
        out_shape=jax.ShapeDtypeStruct((128, NCLASS * 128), BF),
        compiler_params=params(),
        name="place",
    )(inverses)

    dma = pltpu.SemaphoreType.DMA
    fixed = in_hbm(lines)
    piece_shape = jax.ShapeDtypeStruct((3, 4, 16, 16, 128), BF)
    (piece,) = call(cut_kernel, "cut", [smem, hbm], (pos, fixed), [piece_shape], [dma((3, 4))])
    piece = lax.ppermute(piece, "core", [(0, 1), (1, 0)])
    packed = call(
        pack_kernel, "pack", [smem, hbm, vmem], (pos, fixed, piece), [mode_shape] * 4,
        [pltpu.VMEM((3, 4, 16, 16, 128), BF), dma((3, 4))],
    )
    first = [along_z(packed[step], step, EARLY) for step in (1, 2, 3)]
    token = sum(block[0, 0, 0, 0, :, :128].astype(jnp.float32) for block in first[:1]).astype(BF)
    token = lax.ppermute(token, "core", [(EARLY, 1 - EARLY)])
    held = call(hold_kernel, "hold", [free] * 4, (token, *packed[1:]), [mode_shape] * 3, [], {1: 0, 2: 1, 3: 2}, free)
    second = [along_z(held[step - 1], step, 1 - EARLY) for step in (1, 2, 3)]
    (spread,) = call(
        synth_kernel, "synth", [smem] + [vmem] * 7 + [hbm], (pos, packed[0], *first, *second, z_basis), [plane_shape],
        [pltpu.VMEM((2, 768, 512), BF), *z_scratch],
    )
    (folded,) = call(
        functools.partial(middle_kernel, scale=scale_x), "middle", [vmem, hbm, hbm],
        (plane(spread), x_synth, x_fold), [plane_shape],
        [
            pltpu.VMEM((2, 512, 1152), BF), pltpu.VMEM((2, HALF, 1152), BF),
            pltpu.VMEM((2, HALF, 512), BF), pltpu.VMEM((2, 512, HALF), BF), dma((2,)),
        ],
    )
    (modes,) = call(
        functools.partial(analyse_kernel, scale=scale_z), "analyse", [smem, vmem, hbm],
        (pos, plane(folded), z_basis), [jax.ShapeDtypeStruct((4, *mode_shape.shape), BF)],
        [pltpu.VMEM((2, 768, HALF), BF), *z_scratch],
    )
    modes = lax.all_to_all(modes, COLUMN, split_axis=0, concat_axis=0, tiled=True)
    (other,) = call(gather_kernel, "gather", [vmem], (modes,), [jax.ShapeDtypeStruct((4, 3, 4, 2, 16, 256), BF)], [])
    other = lax.ppermute(other, "core", [(0, 1), (1, 0)])
    (solved,) = call(
        solve_kernel, "solve", [smem] * 2 + [vmem] * 5,
        (pos, keep_count, modes, other, lines, operators, class_index),
        [jax.ShapeDtypeStruct((3, 16, 128, 128), jnp.float32)],
        [pltpu.VMEM((8, 128, 768), BF), pltpu.VMEM((3, 16, 128, 128), jnp.float32), dma((3, 8))],
        out_spec=free,
    )
    return solved.reshape(3, 16, NY, 2, 2, 128).transpose(0, 1, 2, 4, 3, 5).reshape(3, 16, NY, 2, 256)


def solution(mesh):
    fine = Mesh(mesh.devices.reshape(4, 2, 4, 2, 2), ("x", "zl", "y", "zh", "core"))
    wide, narrow = ("x", "zl", "y"), ("zh", "core")
    in_specs = (P(None, wide, None, None, narrow), P(), P(wide, narrow), P(wide))
    out_specs = P(None, wide, None, None, narrow)
    return jax.shard_map(body, mesh=fine, in_specs=in_specs, out_specs=out_specs, check_vma=False)
```

```python
import functools
import math

import jax
import jax.numpy as jnp
import ml_dtypes
import numpy as np
from jax import lax
from jax.experimental import pallas as pl
from jax.experimental.pallas import tpu as pltpu
from jax.sharding import Mesh
from jax.sharding import PartitionSpec as P

KX = 512
KZ = 1024
NCLASS = 8
PX = 1536
PZ = 1536
HALF = PX // 2
NY = 32
BF = jnp.bfloat16
VMEM = 28 * 1024 * 1024
COLUMN = ("zl", "zh")
EARLY = 1
ORDER = (1, 0, 2)

def angles(wavenumbers, points, period):
    phases = (wavenumbers[:, None] * points[None, :]) % period
    scaled = np.float32(2.0 * math.pi / period) * phases.astype(np.float32)
    return scaled.astype(np.float64)


def z_tables():
    tables = []
    for parity in range(2):
        index = np.arange(parity, KZ, 2)
        wavenumber = np.where(index < KZ // 2, index, index - KZ)
        theta = angles(wavenumber, np.arange(HALF), PZ)
        tables.append(np.stack([np.cos(theta), np.sin(theta)]))
    return np.stack(tables).astype(np.float32).astype(ml_dtypes.bfloat16)


def x_tables():
    x, y, zl, i = np.meshgrid(np.arange(4), np.arange(4), np.arange(2), np.arange(8), indexing="ij")
    synth, fold = [], []
    for parity in range(2):
        kx = (x * 8 + zl * 4 + y) * 16 + 2 * i + parity
        theta = angles(kx.reshape(-1), np.arange(HALF), PX).reshape(4, 4, 2, 8, HALF)
        basis = np.stack([np.cos(theta), -np.sin(theta)], axis=2).astype(np.float32)
        weight = np.where(kx == 0, 1.0, 2.0).astype(np.float32)[:, :, None, :, :, None]
        synth.append((weight * basis).reshape(512, HALF).T)
        fold.append(basis.reshape(512, HALF))
    return (
        np.stack(synth).astype(ml_dtypes.bfloat16),
        np.stack(fold).astype(ml_dtypes.bfloat16),
    )


def mover(turned):
    row, column = (lax.broadcasted_iota(jnp.int32, (256, 256), axis) for axis in (turned, 1 - turned))
    kx = ((row & 7) << 1) | ((row >> 3) & 1)
    source = (kx << 4) | (((row >> 5) & 3) << 2) | ((row >> 7) << 1) | ((row >> 4) & 1)
    return (column == source).astype(jnp.float32).astype(BF)


def sorter(turned):
    row, column = (lax.broadcasted_iota(jnp.int32, (256, 256), axis) for axis in (turned, 1 - turned))
    return (row == (((column & 127) << 1) | (column >> 7))).astype(jnp.float32).astype(BF)


def wait(copies):
    for copy in copies:
        copy.wait()


def dot(a, b):
    return jnp.dot(a, b, preferred_element_type=jnp.float32)


def place_kernel(inv_ref, w_ref):
    row, column = (lax.broadcasted_iota(jnp.int32, (128, 128), axis) for axis in range(2))
    same = row % 4 == column % 4
    tall = (row[:, :32] // 4 == column[:, :32]).astype(BF)
    wide = (lax.broadcasted_iota(jnp.int32, (32, 128), 0) == lax.broadcasted_iota(jnp.int32, (32, 128), 1) // 4).astype(BF)
    for index in range(NCLASS):
        rows = dot(tall, inv_ref[index]).astype(BF)
        w_ref[:, index * 128 : index * 128 + 128] = jnp.where(same, dot(rows, wide), 0.0).astype(BF)


def pack_kernel(pos, v_hbm, *refs, half):
    outs, (v_ref, sems) = refs[-6:-2], refs[-2:]
    copies = []
    for c in range(3):
        for z in range(4):
            first = pl.multiple_of(z * 32 + pos[3] * 16, 16)
            copies.append(pltpu.make_async_copy(v_hbm.at[c, :, pl.ds(first, 16)], v_ref.at[c, z], sems.at[c, z]))
            copies[-1].start()
    move, sort = mover(0), sorter(0)
    wait(copies)
    parts = []
    for step in range(4):
        z = lax.rem(pos[2] + step, 4)
        parts += [v_ref[c, z].reshape(256, 128) for c in range(3)]
    moved = dot(move, jnp.concatenate(parts, axis=1)).astype(BF)
    parts = []
    for i in range(12):
        part = moved[:, i * 128 : i * 128 + 128]
        parts.append(jnp.concatenate([part[:128], part[128:]], axis=1))
    moved = dot(jnp.concatenate(parts, axis=0), sort).astype(BF)
    for step in range(4):
        outs[step][half] = moved[step * 384 : (step + 1) * 384].reshape(3, 4, 2, 16, 256)


def hold_kernel(*refs):
    pass


def preload_kernel(after_ref, inv_ref, *refs):
    copies = [pltpu.make_async_copy(refs[i], refs[3 + i], refs[7].at[i]) for i in range(3)]
    for copy in copies:
        copy.start()
    place_kernel(inv_ref, refs[6])
    wait(copies)


def gather_kernel(n_ref, out_ref):
    out_ref[...] = n_ref[:, 1]


def z_copies(table_hbm, table_ref, sems):
    return [pltpu.make_async_copy(table_hbm.at[p], table_ref.at[p], sems.at[p]) for p in range(2)]


def synth_kernel(pos, r0, e1, e2, e3, l1, l2, l3, table_ref, out_ref, lhs):
    nc = 3

    def fill(step, block):
        z = lax.rem(pos[2] + 4 - step, 4)
        for core in range(2):
            quarter = (z // 2) * 2 + lax.rem(pos[3] + core, 2)
            lanes = pl.ds(pl.multiple_of(quarter * 128, 128), 128)
            for ri in range(2):
                rows = pl.ds(pl.multiple_of(ri * (128 * nc) + lax.rem(z, 2) * (64 * nc), 64), 64 * nc)
                part = block[core, :, :, ri].reshape(64 * nc, 256)
                for parity in range(2):
                    lhs[parity, rows, lanes] = part[:, parity * 128 : parity * 128 + 128]

    fill(0, r0)

    @pl.when(pos[3] == EARLY)
    def _():
        for step, block in enumerate((e1, e2, e3)):
            fill(step + 1, block)

    @pl.when(pos[3] != EARLY)
    def _():
        for step, block in enumerate((l1, l2, l3)):
            fill(step + 1, block)

    n = 128 * nc
    sums = []
    for parity in range(2):
        by_cos = dot(lhs[parity], table_ref[parity, 0])
        by_sin = dot(lhs[parity], table_ref[parity, 1])
        sums.append((by_cos[:n] - by_sin[n:], by_sin[:n] + by_cos[n:]))
    for ri in range(2):
        even, odd = sums[0][ri], sums[1][ri]
        for half, both in enumerate((even + odd, even - odd)):
            part = both.reshape(2, nc, 4, 2, 8, HALF)
            for plane in range(4):
                for c in range(nc):
                    mixed = [part[zl, c, plane, parity] for parity in range(2) for zl in range(2)]
                    mixed = jnp.concatenate(mixed, axis=0).astype(BF)
                    for quarter in range(2):
                        out_ref[plane * 4 + half * 2 + quarter, c, ri] = mixed[:, quarter * 384 : quarter * 384 + 384]


def middle_kernel(d_ref, synth_ref, fold_ref, table_hbm, out_ref, table_ref, data, prod, sem, *, scale):
    table_copy = pltpu.make_async_copy(table_hbm, table_ref, sem)
    table_copy.start()
    for parity in range(2):
        for c in range(3):
            part = d_ref[:, c, :, parity * 16 : parity * 16 + 16, :].reshape(512, 384)
            data[parity, :, c * 384 : c * 384 + 384] = part
    for step in range(3):
        rows = slice(step * 256, step * 256 + 256)
        even = dot(synth_ref[0, rows, :], data[0])
        odd = dot(synth_ref[1, rows, :], data[1])
        low, high = even + odd, even - odd
        for c in range(3):
            lanes = slice(c * 384, c * 384 + 384)
            one, two = low[:, lanes] * low[:, 384:768], high[:, lanes] * high[:, 384:768]
            prod[0, rows, lanes] = (one + two).astype(BF)
            prod[1, rows, lanes] = (one - two).astype(BF)
    for parity in range(2):
        spectra = (dot(fold_ref[parity], prod[parity]) * scale).astype(BF)
        for c in range(3):
            part = spectra[:, c * 384 : c * 384 + 384].reshape(16, 2, 16, 384)
            out_ref[:, c, :, parity * 16 : parity * 16 + 16, :] = part
    table_copy.wait()


def analyse_kernel(pos, b_ref, table_ref, out_ref, lhs, *, scale):
    nc = 3
    n = 128 * nc
    for plane in range(4):
        for quarter in range(2):
            for ri in range(2):
                low = b_ref[plane * 4 + quarter, :, ri].reshape(32 * nc, 384).astype(jnp.float32)
                high = b_ref[plane * 4 + quarter + 2, :, ri].reshape(32 * nc, 384).astype(jnp.float32)
                rows = slice(ri * n + plane * 32 * nc, ri * n + plane * 32 * nc + 32 * nc)
                lanes = slice(quarter * 384, quarter * 384 + 384)
                lhs[0, rows, lanes] = (low + high).astype(BF)
                lhs[1, rows, lanes] = (low - high).astype(BF)
    for parity in range(2):
        by_cos, by_sin = (
            lax.dot_general(
                lhs[parity], table_ref[parity, i], (((1,), (1,)), ((), ())), preferred_element_type=jnp.float32
            )
            for i in range(2)
        )
        for ri, spectra in enumerate((by_cos[:n] + by_sin[n:], by_cos[n:] - by_sin[:n])):
            part = (spectra * scale).reshape(4, nc, 2, 2, 8, 512)
            for zl in range(2):
                for quarter in range(4):
                    for plane in range(4):
                        for c in range(nc):
                            piece = part[plane, c, :, zl, :, quarter * 128 : quarter * 128 + 128]
                            block, other = zl * 2 + quarter // 2, lax.rem(quarter + pos[3], 2)
                            lanes = slice(parity * 128, parity * 128 + 128)
                            out_ref[block, other, c, plane, ri, :, lanes] = piece.reshape(16, 128).astype(BF)


def right_rows(pos, count_ref, blocks, other, v_ref, store):
    move, sort = mover(1), sorter(1)
    row = lax.broadcasted_iota(jnp.int32, (16, 16, 128), 1)
    kx = lax.broadcasted_iota(jnp.int32, (16, 16, 128), 0)
    lane = lax.broadcasted_iota(jnp.int32, (16, 16, 128), 2)
    index = ((pos[2] // 2) * 2 + pos[3]) * 256 + lane + 128 * (lax.rem(row, 4) // 2)
    wavenumber = jnp.where(index < KZ // 2, index, index - KZ)
    counts = jnp.concatenate([jnp.full((1, 16, 128), count_ref[k], jnp.int32) for k in range(16)], axis=0)
    mean = (kx + pos[4] == 0) & (wavenumber == 0)
    half = jnp.where((jnp.abs(wavenumber) < counts) & jnp.logical_not(mean), 0.5, 0.0).astype(jnp.float32)
    both = dot(jnp.concatenate([block.reshape(128, 256) for block in blocks], axis=0), sort).astype(BF)
    both = [both[i * 128 : i * 128 + 128] for i in range(12)]
    both = [jnp.concatenate([part[:, :128], part[:, 128:]], axis=0) for part in both]
    moved = dot(move, jnp.concatenate(both, axis=1))
    for place in range(4):
        z = (place % 2) * 2 + place // 2
        rows = pl.ds(pl.multiple_of((z * 2 + lax.rem(pos[3] + other, 2)) * 16, 16), 16)
        for c in range(3):
            old = v_ref[c, :, rows, :].astype(jnp.float32)
            lanes = slice((place * 3 + c) * 128, (place * 3 + c) * 128 + 128)
            new = (old + moved[:, lanes].reshape(16, 16, 128) * half).astype(BF)
            for k in range(16):
                store(rows, place, c, k, new[k])


def right_kernel(pos, count_ref, n_ref, v_ref, out_ref):
    def store(rows, place, c, k, value):
        out_ref[k // 2, place, :, (c * 2 + k % 2) * 128 : (c * 2 + k % 2) * 128 + 128] = value

    right_rows(pos, count_ref, [n_ref[place, 0, c] for place in range(4) for c in range(3)], 0, v_ref, store)


def solve_kernel(pos, count_ref, right_ref, other_ref, v_ref, w_ref, class_ref, out_ref, right, done, sems):
    def store(rows, place, c, k, value):
        right[k // 2, rows, (c * 2 + k % 2) * 128 : (c * 2 + k % 2) * 128 + 128] = value

    right_rows(pos, count_ref, [other_ref[place, c] for place in range(4) for c in range(3)], 1, v_ref, store)
    for place in range(4):
        z = (place % 2) * 2 + place // 2
        rows = pl.ds(pl.multiple_of((z * 2 + pos[3]) * 16, 16), 16)
        for pair in range(8):
            right[pair, rows, :] = right_ref[pair, place]
    early = (lax.broadcasted_iota(jnp.int32, (16, 128), 0) & 3) < 2
    copies = []
    for pair in range(8):
        classes = []
        for k in range(2):
            line = class_ref[pair * 2 + k : pair * 2 + k + 1, :]
            classes.append(jnp.where(early, line[:, :128], line[:, 128:]))
        classes = jnp.concatenate(classes * 3, axis=1)
        line = right[pair].reshape(8, 16, 768)
        masked = []
        for index in range(NCLASS):
            chosen = (classes == index).astype(jnp.float32).astype(BF)
            masked.append((line * chosen[None]).reshape(128, 768))
        total = dot(w_ref[...], jnp.concatenate(masked, axis=0))
        block = pl.ds(pair * 2, 2)
        for c in range(3):
            for k in range(2):
                done[c, pair * 2 + k] = total[:, (c * 2 + k) * 128 : (c * 2 + k) * 128 + 128]
            copies.append(pltpu.make_async_copy(done.at[c, block], out_ref.at[c, block], sems.at[c, pair]))
            copies[-1].start()
    wait(copies)


def params():
    return pltpu.CompilerParams(vmem_limit_bytes=VMEM)


def in_hbm(array):
    return pltpu.with_memory_space_constraint(array, pltpu.HBM)


def spec(memory):
    return pl.BlockSpec(memory_space=memory)


def along_z(block, step, core):
    pairs = []
    for z in range(4):
        to = (z + step) % 4
        pairs.append((((z % 2) * 2 + z // 2) * 2 + core, ((to % 2) * 2 + to // 2) * 2 + core))
    return lax.ppermute(block, ("zl", "zh", "core"), pairs)


def plane(blocks):
    return lax.all_to_all(blocks, ("x", "y"), split_axis=0, concat_axis=0, tiled=True)


def after(value, *earlier):
    return lax.optimization_barrier((value, *earlier))[0]


def body(velocity, inverses, class_index, keep_count):
    scale_x = (0.5 / math.sqrt(KX * KZ)) ** 2 / PX
    scale_z = 2.0 * math.sqrt(KX * KZ) / PZ
    z_basis, x_synth, x_fold = (in_hbm(jnp.asarray(t)) for t in (z_tables(), *x_tables()))
    z_scratch = [pltpu.VMEM((2, 2, 512, HALF), BF), pltpu.SemaphoreType.DMA((2,))]
    lines = velocity.reshape(3, 16, NY, 2, 2, 128).transpose(0, 1, 2, 4, 3, 5).reshape(3, 16, 128, 128)
    x, y, zl = (lax.axis_index(name) for name in ("x", "y", "zl"))
    pos = jnp.stack([x, y, lax.axis_index("zh") * 2 + zl, lax.axis_index("core"), (x * 8 + zl * 4 + y) * 16])

    mode_shape = jax.ShapeDtypeStruct((2, 3, 4, 2, 16, 256), BF)
    plane_shape = jax.ShapeDtypeStruct((16, 3, 2, 32, 384), BF)
    table_shape = pltpu.VMEM((2, 2, 512, HALF), BF)
    smem, vmem, hbm, free = (spec(m) for m in (pltpu.SMEM, pltpu.VMEM, pltpu.HBM, pl.ANY))

    def call(kernel, name, specs, args, outs, scratch, aliases={}, out_spec=vmem):
        return pl.pallas_call(
            kernel,
            in_specs=specs,
            out_specs=[out_spec] * len(outs),
            out_shape=outs,
            scratch_shapes=scratch,
            input_output_aliases=aliases,
            compiler_params=params(),
            name=name,
        )(*args)

    dma = pltpu.SemaphoreType.DMA
    fixed = in_hbm(lines)
    other = lax.ppermute(velocity, "core", [(0, 1), (1, 0)])
    other = other.reshape(3, 16, NY, 2, 2, 128).transpose(0, 1, 2, 4, 3, 5).reshape(3, 16, 128, 128)
    scratch = [pltpu.VMEM((3, 4, 16, 16, 128), BF), dma((3, 4))]
    packed = call(
        functools.partial(pack_kernel, half=0), "pack", [smem, hbm], (pos, fixed), [mode_shape] * 4, scratch
    )
    packed = call(
        functools.partial(pack_kernel, half=1), "pack", [smem, free] + [vmem] * 4, (pos, other, *packed),
        [mode_shape] * 4, scratch, {2: 0, 3: 1, 4: 2, 5: 3},
    )
    first = [along_z(packed[step], step, EARLY) for step in (1, 2, 3)]
    table, *x_held, operators = call(
        preload_kernel, "preload", [free, vmem] + [hbm] * 3, (packed[0], inverses, z_basis, x_synth, x_fold),
        [
            table_shape, pltpu.VMEM((2, HALF, 512), BF), pltpu.VMEM((2, 512, HALF), BF),
            jax.ShapeDtypeStruct((128, NCLASS * 128), BF),
        ],
        [dma((3,))],
    )
    token = first[0][0, 0, 0, 0, :, :128]
    token = lax.ppermute(token, "core", [(EARLY, 1 - EARLY)])
    held = call(
        hold_kernel, "hold", [free] * 5, (token, table, packed[1], packed[2], packed[3]), [mode_shape] * 3, [],
        {2: 0, 3: 1, 4: 2}, free,
    )
    ready = {1: held[0], 2: held[1], 3: held[2]}
    second = [along_z(ready[step], step, 1 - EARLY) for step in (1, 2, 3)]
    (spread,) = call(
        synth_kernel, "synth", [smem] + [vmem] * 8, (pos, packed[0], *first, *second, table), [plane_shape],
        [pltpu.VMEM((2, 768, 512), BF)],
    )
    folded, table = call(
        functools.partial(middle_kernel, scale=scale_x), "middle", [vmem] * 3 + [hbm],
        (plane(spread), *x_held, z_basis), [plane_shape, table_shape],
        [
            pltpu.VMEM((2, 512, 1152), BF), pltpu.VMEM((2, HALF, 1152), BF), dma(()),
        ],
    )
    (modes,) = call(
        functools.partial(analyse_kernel, scale=scale_z), "analyse", [smem, vmem, vmem],
        (pos, plane(folded), table), [jax.ShapeDtypeStruct((4, *mode_shape.shape), BF)],
        [pltpu.VMEM((2, 768, HALF), BF)],
    )
    modes = lax.all_to_all(modes, COLUMN, split_axis=0, concat_axis=0, tiled=True)
    (other,) = call(gather_kernel, "gather", [vmem], (modes,), [jax.ShapeDtypeStruct((4, 3, 4, 2, 16, 256), BF)], [])
    other = lax.ppermute(other, "core", [(0, 1), (1, 0)])
    (right,) = call(
        right_kernel, "right", [smem] * 2 + [vmem] * 2, (pos, keep_count, modes, lines),
        [jax.ShapeDtypeStruct((8, 4, 16, 768), BF)], [],
    )
    (solved,) = call(
        solve_kernel, "solve", [smem] * 2 + [vmem] * 5,
        (pos, keep_count, right, other, lines, operators, class_index),
        [jax.ShapeDtypeStruct((3, 16, 128, 128), jnp.float32)],
        [pltpu.VMEM((8, 128, 768), BF), pltpu.VMEM((3, 16, 128, 128), jnp.float32), dma((3, 8))],
        out_spec=free,
    )
    return solved.reshape(3, 16, NY, 2, 2, 128).transpose(0, 1, 2, 4, 3, 5).reshape(3, 16, NY, 2, 256)


def solution(mesh):
    fine = Mesh(mesh.devices.reshape(4, 2, 4, 2, 2), ("x", "zl", "y", "zh", "core"))
    wide, narrow = ("x", "zl", "y"), ("zh", "core")
    in_specs = (P(None, wide, None, None, narrow), P(), P(wide, narrow), P(wide))
    out_specs = P(None, wide, None, None, narrow)
    return jax.shard_map(body, mesh=fine, in_specs=in_specs, out_specs=out_specs, check_vma=False)
```

```python
import functools
import math

import jax
import jax.numpy as jnp
import ml_dtypes
import numpy as np
from jax import lax
from jax.experimental import pallas as pl
from jax.experimental.pallas import tpu as pltpu
from jax.sharding import Mesh
from jax.sharding import PartitionSpec as P

KX = 512
KZ = 1024
NCLASS = 8
PX = 1536
PZ = 1536
HALF = PX // 2
NY = 32
BF = jnp.bfloat16
VMEM = 28 * 1024 * 1024
COLUMN = ("zl", "zh")
EARLY = 1
ORDER = (1, 0, 2)

def angles(wavenumbers, points, period):
    phases = (wavenumbers[:, None] * points[None, :]) % period
    scaled = np.float32(2.0 * math.pi / period) * phases.astype(np.float32)
    return scaled.astype(np.float64)


def z_tables():
    tables = []
    for parity in range(2):
        index = np.arange(parity, KZ, 2)
        wavenumber = np.where(index < KZ // 2, index, index - KZ)
        theta = angles(wavenumber, np.arange(HALF), PZ)
        tables.append(np.stack([np.cos(theta), np.sin(theta)]))
    return np.stack(tables).astype(np.float32).astype(ml_dtypes.bfloat16)


def x_tables():
    x, y, zl, i = np.meshgrid(np.arange(4), np.arange(4), np.arange(2), np.arange(8), indexing="ij")
    synth, fold = [], []
    for parity in range(2):
        kx = (x * 8 + zl * 4 + y) * 16 + 2 * i + parity
        theta = angles(kx.reshape(-1), np.arange(HALF), PX).reshape(4, 4, 2, 8, HALF)
        basis = np.stack([np.cos(theta), -np.sin(theta)], axis=2).astype(np.float32)
        weight = np.where(kx == 0, 1.0, 2.0).astype(np.float32)[:, :, None, :, :, None]
        synth.append((weight * basis).reshape(512, HALF).T)
        fold.append(basis.reshape(512, HALF))
    return (
        np.stack(synth).astype(ml_dtypes.bfloat16),
        np.stack(fold).astype(ml_dtypes.bfloat16),
    )


def mover(turned):
    row, column = (lax.broadcasted_iota(jnp.int32, (256, 256), axis) for axis in (turned, 1 - turned))
    kx = ((row & 7) << 1) | ((row >> 3) & 1)
    source = (kx << 4) | (((row >> 5) & 3) << 2) | ((row >> 7) << 1) | ((row >> 4) & 1)
    return (column == source).astype(jnp.float32).astype(BF)


def sorter(turned):
    row, column = (lax.broadcasted_iota(jnp.int32, (256, 256), axis) for axis in (turned, 1 - turned))
    return (row == (((column & 127) << 1) | (column >> 7))).astype(jnp.float32).astype(BF)


def wait(copies):
    for copy in copies:
        copy.wait()


def dot(a, b):
    return jnp.dot(a, b, preferred_element_type=jnp.float32)


def place_kernel(inv_ref, w_ref):
    row, column = (lax.broadcasted_iota(jnp.int32, (128, 128), axis) for axis in range(2))
    same = row % 4 == column % 4
    tall = (row[:, :32] // 4 == column[:, :32]).astype(BF)
    wide = (lax.broadcasted_iota(jnp.int32, (32, 128), 0) == lax.broadcasted_iota(jnp.int32, (32, 128), 1) // 4).astype(BF)
    for index in range(NCLASS):
        rows = dot(tall, inv_ref[index]).astype(BF)
        w_ref[:, index * 128 : index * 128 + 128] = jnp.where(same, dot(rows, wide), 0.0).astype(BF)


def pack_kernel(pos, v_hbm, *refs, half):
    own, outs, (v_ref, sems) = refs[:-6], refs[-6:-2], refs[-2:]
    copies = []
    for c in range(3):
        for z in range(4):
            first = pl.multiple_of(z * 32 + pos[3] * 16, 16)
            copies.append(pltpu.make_async_copy(v_hbm.at[c, :, pl.ds(first, 16)], v_ref.at[c, z], sems.at[c, z]))
            copies[-1].start()
    move, sort = mover(0), sorter(0)
    wait(copies)
    parts = []
    for step in range(4):
        z = lax.rem(pos[2] + step, 4)
        parts += [v_ref[c, z].reshape(256, 128) for c in range(3)]
    moved = dot(move, jnp.concatenate(parts, axis=1)).astype(BF)
    parts = []
    for i in range(12):
        part = moved[:, i * 128 : i * 128 + 128]
        parts.append(jnp.concatenate([part[:128], part[128:]], axis=1))
    moved = dot(jnp.concatenate(parts, axis=0), sort).astype(BF)
    for step in range(4):
        if half:
            outs[step][0] = own[step][0]
        outs[step][half] = moved[step * 384 : (step + 1) * 384].reshape(3, 4, 2, 16, 256)


def hold_kernel(*refs):
    pass


def preload_kernel(after_ref, inv_ref, *refs):
    copies = [pltpu.make_async_copy(refs[i], refs[3 + i], refs[7].at[i]) for i in range(3)]
    for copy in copies:
        copy.start()
    place_kernel(inv_ref, refs[6])
    wait(copies)


def gather_kernel(n_ref, out_ref):
    out_ref[...] = n_ref[:, 1]


def z_copies(table_hbm, table_ref, sems):
    return [pltpu.make_async_copy(table_hbm.at[p], table_ref.at[p], sems.at[p]) for p in range(2)]


def synth_kernel(pos, r0, e1, e2, e3, l1, l2, l3, table_ref, out_ref, lhs):
    nc = 3

    def fill(step, block):
        z = lax.rem(pos[2] + 4 - step, 4)
        for core in range(2):
            quarter = (z // 2) * 2 + lax.rem(pos[3] + core, 2)
            lanes = pl.ds(pl.multiple_of(quarter * 128, 128), 128)
            for ri in range(2):
                rows = pl.ds(pl.multiple_of(ri * (128 * nc) + lax.rem(z, 2) * (64 * nc), 64), 64 * nc)
                part = block[core, :, :, ri].reshape(64 * nc, 256)
                for parity in range(2):
                    lhs[parity, rows, lanes] = part[:, parity * 128 : parity * 128 + 128]

    fill(0, r0)

    @pl.when(pos[3] == EARLY)
    def _():
        for step, block in enumerate((e1, e2, e3)):
            fill(step + 1, block)

    @pl.when(pos[3] != EARLY)
    def _():
        for step, block in enumerate((l1, l2, l3)):
            fill(step + 1, block)

    n = 128 * nc
    sums = []
    for parity in range(2):
        by_cos = dot(lhs[parity], table_ref[parity, 0])
        by_sin = dot(lhs[parity], table_ref[parity, 1])
        sums.append((by_cos[:n] - by_sin[n:], by_sin[:n] + by_cos[n:]))
    for ri in range(2):
        even, odd = sums[0][ri], sums[1][ri]
        for half, both in enumerate((even + odd, even - odd)):
            part = both.reshape(2, nc, 4, 2, 8, HALF)
            for plane in range(4):
                for c in range(nc):
                    mixed = [part[zl, c, plane, parity] for parity in range(2) for zl in range(2)]
                    mixed = jnp.concatenate(mixed, axis=0).astype(BF)
                    for quarter in range(2):
                        out_ref[plane * 4 + half * 2 + quarter, c, ri] = mixed[:, quarter * 384 : quarter * 384 + 384]


def middle_kernel(d_ref, synth_ref, fold_ref, table_hbm, out_ref, table_ref, data, prod, sem, *, scale):
    table_copy = pltpu.make_async_copy(table_hbm, table_ref, sem)
    table_copy.start()
    for parity in range(2):
        for c in range(3):
            part = d_ref[:, c, :, parity * 16 : parity * 16 + 16, :].reshape(512, 384)
            data[parity, :, c * 384 : c * 384 + 384] = part
    for step in range(3):
        rows = slice(step * 256, step * 256 + 256)
        even = dot(synth_ref[0, rows, :], data[0])
        odd = dot(synth_ref[1, rows, :], data[1])
        low, high = even + odd, even - odd
        for c in range(3):
            lanes = slice(c * 384, c * 384 + 384)
            one, two = low[:, lanes] * low[:, 384:768], high[:, lanes] * high[:, 384:768]
            prod[0, rows, lanes] = (one + two).astype(BF)
            prod[1, rows, lanes] = (one - two).astype(BF)
    for parity in range(2):
        spectra = (dot(fold_ref[parity], prod[parity]) * scale).astype(BF)
        for c in range(3):
            part = spectra[:, c * 384 : c * 384 + 384].reshape(16, 2, 16, 384)
            out_ref[:, c, :, parity * 16 : parity * 16 + 16, :] = part
    table_copy.wait()


def analyse_kernel(pos, b_ref, table_ref, out_ref, lhs, *, scale):
    nc = 3
    n = 128 * nc
    for plane in range(4):
        for quarter in range(2):
            for ri in range(2):
                low = b_ref[plane * 4 + quarter, :, ri].reshape(32 * nc, 384).astype(jnp.float32)
                high = b_ref[plane * 4 + quarter + 2, :, ri].reshape(32 * nc, 384).astype(jnp.float32)
                rows = slice(ri * n + plane * 32 * nc, ri * n + plane * 32 * nc + 32 * nc)
                lanes = slice(quarter * 384, quarter * 384 + 384)
                lhs[0, rows, lanes] = (low + high).astype(BF)
                lhs[1, rows, lanes] = (low - high).astype(BF)
    for parity in range(2):
        by_cos, by_sin = (
            lax.dot_general(
                lhs[parity], table_ref[parity, i], (((1,), (1,)), ((), ())), preferred_element_type=jnp.float32
            )
            for i in range(2)
        )
        for ri, spectra in enumerate((by_cos[:n] + by_sin[n:], by_cos[n:] - by_sin[:n])):
            part = (spectra * scale).reshape(4, nc, 2, 2, 8, 512)
            for zl in range(2):
                for quarter in range(4):
                    for plane in range(4):
                        for c in range(nc):
                            piece = part[plane, c, :, zl, :, quarter * 128 : quarter * 128 + 128]
                            block, other = zl * 2 + quarter // 2, lax.rem(quarter + pos[3], 2)
                            lanes = slice(parity * 128, parity * 128 + 128)
                            out_ref[block, other, c, plane, ri, :, lanes] = piece.reshape(16, 128).astype(BF)


def right_rows(pos, count_ref, blocks, other, v_ref, store):
    move, sort = mover(1), sorter(1)
    row = lax.broadcasted_iota(jnp.int32, (16, 16, 128), 1)
    kx = lax.broadcasted_iota(jnp.int32, (16, 16, 128), 0)
    lane = lax.broadcasted_iota(jnp.int32, (16, 16, 128), 2)
    index = ((pos[2] // 2) * 2 + pos[3]) * 256 + lane + 128 * (lax.rem(row, 4) // 2)
    wavenumber = jnp.where(index < KZ // 2, index, index - KZ)
    counts = jnp.concatenate([jnp.full((1, 16, 128), count_ref[k], jnp.int32) for k in range(16)], axis=0)
    mean = (kx + pos[4] == 0) & (wavenumber == 0)
    half = jnp.where((jnp.abs(wavenumber) < counts) & jnp.logical_not(mean), 0.5, 0.0).astype(jnp.float32)
    both = dot(jnp.concatenate([block.reshape(128, 256) for block in blocks], axis=0), sort).astype(BF)
    both = [both[i * 128 : i * 128 + 128] for i in range(12)]
    both = [jnp.concatenate([part[:, :128], part[:, 128:]], axis=0) for part in both]
    moved = dot(move, jnp.concatenate(both, axis=1))
    for place in range(4):
        z = (place % 2) * 2 + place // 2
        rows = pl.ds(pl.multiple_of((z * 2 + lax.rem(pos[3] + other, 2)) * 16, 16), 16)
        for c in range(3):
            old = v_ref[c, :, rows, :].astype(jnp.float32)
            lanes = slice((place * 3 + c) * 128, (place * 3 + c) * 128 + 128)
            new = (old + moved[:, lanes].reshape(16, 16, 128) * half).astype(BF)
            for k in range(16):
                store(rows, place, c, k, new[k])


def right_kernel(pos, count_ref, n_ref, v_ref, out_ref):
    def store(rows, place, c, k, value):
        out_ref[k // 2, place, :, (c * 2 + k % 2) * 128 : (c * 2 + k % 2) * 128 + 128] = value

    right_rows(pos, count_ref, [n_ref[place, 0, c] for place in range(4) for c in range(3)], 0, v_ref, store)


def solve_kernel(pos, count_ref, right_ref, other_ref, v_ref, w_ref, class_ref, out_ref, right, done, sems):
    def store(rows, place, c, k, value):
        right[k // 2, rows, (c * 2 + k % 2) * 128 : (c * 2 + k % 2) * 128 + 128] = value

    right_rows(pos, count_ref, [other_ref[place, c] for place in range(4) for c in range(3)], 1, v_ref, store)
    for place in range(4):
        z = (place % 2) * 2 + place // 2
        rows = pl.ds(pl.multiple_of((z * 2 + pos[3]) * 16, 16), 16)
        for pair in range(8):
            right[pair, rows, :] = right_ref[pair, place]
    early = (lax.broadcasted_iota(jnp.int32, (16, 128), 0) & 3) < 2
    copies = []
    for pair in range(8):
        classes = []
        for k in range(2):
            line = class_ref[pair * 2 + k : pair * 2 + k + 1, :]
            classes.append(jnp.where(early, line[:, :128], line[:, 128:]))
        classes = jnp.concatenate(classes * 3, axis=1)
        line = right[pair].reshape(8, 16, 768)
        masked = []
        for index in range(NCLASS):
            chosen = (classes == index).astype(jnp.float32).astype(BF)
            masked.append((line * chosen[None]).reshape(128, 768))
        total = dot(w_ref[...], jnp.concatenate(masked, axis=0))
        block = pl.ds(pair * 2, 2)
        for c in range(3):
            for k in range(2):
                done[c, pair * 2 + k] = total[:, (c * 2 + k) * 128 : (c * 2 + k) * 128 + 128]
            copies.append(pltpu.make_async_copy(done.at[c, block], out_ref.at[c, block], sems.at[c, pair]))
            copies[-1].start()
    wait(copies)


def params():
    return pltpu.CompilerParams(vmem_limit_bytes=VMEM)


def in_hbm(array):
    return pltpu.with_memory_space_constraint(array, pltpu.HBM)


def spec(memory):
    return pl.BlockSpec(memory_space=memory)


def along_z(block, step, core):
    pairs = []
    for z in range(4):
        to = (z + step) % 4
        pairs.append((((z % 2) * 2 + z // 2) * 2 + core, ((to % 2) * 2 + to // 2) * 2 + core))
    return lax.ppermute(block, ("zl", "zh", "core"), pairs)


def plane(blocks):
    return lax.all_to_all(blocks, ("x", "y"), split_axis=0, concat_axis=0, tiled=True)


def after(value, *earlier):
    return lax.optimization_barrier((value, *earlier))[0]


def body(velocity, inverses, class_index, keep_count):
    scale_x = (0.5 / math.sqrt(KX * KZ)) ** 2 / PX
    scale_z = 2.0 * math.sqrt(KX * KZ) / PZ
    z_basis, x_synth, x_fold = (in_hbm(jnp.asarray(t)) for t in (z_tables(), *x_tables()))
    z_scratch = [pltpu.VMEM((2, 2, 512, HALF), BF), pltpu.SemaphoreType.DMA((2,))]
    lines = velocity.reshape(3, 16, NY, 2, 2, 128).transpose(0, 1, 2, 4, 3, 5).reshape(3, 16, 128, 128)
    x, y, zl = (lax.axis_index(name) for name in ("x", "y", "zl"))
    pos = jnp.stack([x, y, lax.axis_index("zh") * 2 + zl, lax.axis_index("core"), (x * 8 + zl * 4 + y) * 16])

    mode_shape = jax.ShapeDtypeStruct((2, 3, 4, 2, 16, 256), BF)
    plane_shape = jax.ShapeDtypeStruct((16, 3, 2, 32, 384), BF)
    table_shape = pltpu.VMEM((2, 2, 512, HALF), BF)
    smem, vmem, hbm, free = (spec(m) for m in (pltpu.SMEM, pltpu.VMEM, pltpu.HBM, pl.ANY))

    def call(kernel, name, specs, args, outs, scratch, aliases={}, out_spec=vmem):
        return pl.pallas_call(
            kernel,
            in_specs=specs,
            out_specs=[out_spec] * len(outs),
            out_shape=outs,
            scratch_shapes=scratch,
            input_output_aliases=aliases,
            compiler_params=params(),
            name=name,
        )(*args)

    half_shape = jax.ShapeDtypeStruct((1, 3, 4, 2, 16, 256), BF)
    dma = pltpu.SemaphoreType.DMA
    fixed = in_hbm(lines)
    other = lax.ppermute(velocity, "core", [(0, 1), (1, 0)])
    other = other.reshape(3, 16, NY, 2, 2, 128).transpose(0, 1, 2, 4, 3, 5).reshape(3, 16, 128, 128)
    scratch = [pltpu.VMEM((3, 4, 16, 16, 128), BF), dma((3, 4))]
    packed = call(
        functools.partial(pack_kernel, half=0), "pack", [smem, hbm], (pos, fixed), [half_shape] * 4, scratch
    )
    packed = call(
        functools.partial(pack_kernel, half=1), "pack", [smem, free] + [vmem] * 4, (pos, other, *packed),
        [mode_shape] * 4, scratch,
    )
    first = [along_z(packed[step], step, EARLY) for step in (1, 2, 3)]
    table, *x_held, operators = call(
        preload_kernel, "preload", [free, vmem] + [hbm] * 3, (packed[0], inverses, z_basis, x_synth, x_fold),
        [
            table_shape, pltpu.VMEM((2, HALF, 512), BF), pltpu.VMEM((2, 512, HALF), BF),
            jax.ShapeDtypeStruct((128, NCLASS * 128), BF),
        ],
        [dma((3,))],
    )
    token = first[0][0, 0, 0, 0, :, :128]
    token = lax.ppermute(token, "core", [(EARLY, 1 - EARLY)])
    held = call(
        hold_kernel, "hold", [free] * 5, (token, table, packed[1], packed[2], packed[3]), [mode_shape] * 3, [],
        {2: 0, 3: 1, 4: 2}, free,
    )
    ready = {1: held[0], 2: held[1], 3: held[2]}
    second = [along_z(ready[step], step, 1 - EARLY) for step in (1, 2, 3)]
    (spread,) = call(
        synth_kernel, "synth", [smem] + [vmem] * 8, (pos, packed[0], *first, *second, table), [plane_shape],
        [pltpu.VMEM((2, 768, 512), BF)],
    )
    folded, table = call(
        functools.partial(middle_kernel, scale=scale_x), "middle", [vmem] * 3 + [hbm],
        (plane(spread), *x_held, z_basis), [plane_shape, table_shape],
        [
            pltpu.VMEM((2, 512, 1152), BF), pltpu.VMEM((2, HALF, 1152), BF), dma(()),
        ],
    )
    (modes,) = call(
        functools.partial(analyse_kernel, scale=scale_z), "analyse", [smem, vmem, vmem],
        (pos, plane(folded), table), [jax.ShapeDtypeStruct((4, *mode_shape.shape), BF)],
        [pltpu.VMEM((2, 768, HALF), BF)],
    )
    modes = lax.all_to_all(modes, COLUMN, split_axis=0, concat_axis=0, tiled=True)
    (other,) = call(gather_kernel, "gather", [vmem], (modes,), [jax.ShapeDtypeStruct((4, 3, 4, 2, 16, 256), BF)], [])
    other = lax.ppermute(other, "core", [(0, 1), (1, 0)])
    (right,) = call(
        right_kernel, "right", [smem] * 2 + [vmem] * 2, (pos, keep_count, modes, lines),
        [jax.ShapeDtypeStruct((8, 4, 16, 768), BF)], [],
    )
    (solved,) = call(
        solve_kernel, "solve", [smem] * 2 + [vmem] * 5,
        (pos, keep_count, right, other, lines, operators, class_index),
        [jax.ShapeDtypeStruct((3, 16, 128, 128), jnp.float32)],
        [pltpu.VMEM((8, 128, 768), BF), pltpu.VMEM((3, 16, 128, 128), jnp.float32), dma((3, 8))],
        out_spec=free,
    )
    return solved.reshape(3, 16, NY, 2, 2, 128).transpose(0, 1, 2, 4, 3, 5).reshape(3, 16, NY, 2, 256)


def solution(mesh):
    fine = Mesh(mesh.devices.reshape(4, 2, 4, 2, 2), ("x", "zl", "y", "zh", "core"))
    wide, narrow = ("x", "zl", "y"), ("zh", "core")
    in_specs = (P(None, wide, None, None, narrow), P(), P(wide, narrow), P(wide))
    out_specs = P(None, wide, None, None, narrow)
    return jax.shard_map(body, mesh=fine, in_specs=in_specs, out_specs=out_specs, check_vma=False)
```

```python
import functools
import math

import jax
import jax.numpy as jnp
import ml_dtypes
import numpy as np
from jax import lax
from jax.experimental import pallas as pl
from jax.experimental.pallas import tpu as pltpu
from jax.sharding import Mesh
from jax.sharding import PartitionSpec as P

KX = 512
KZ = 1024
NCLASS = 8
PX = 1536
PZ = 1536
HALF = PX // 2
NY = 32
BF = jnp.bfloat16
VMEM = 28 * 1024 * 1024
COLUMN = ("zl", "zh")
EARLY = 1
ORDER = (1, 0, 2)

def angles(wavenumbers, points, period):
    phases = (wavenumbers[:, None] * points[None, :]) % period
    scaled = np.float32(2.0 * math.pi / period) * phases.astype(np.float32)
    return scaled.astype(np.float64)


def z_tables():
    tables = []
    for parity in range(2):
        index = np.arange(parity, KZ, 2)
        wavenumber = np.where(index < KZ // 2, index, index - KZ)
        theta = angles(wavenumber, np.arange(HALF), PZ)
        tables.append(np.stack([np.cos(theta), np.sin(theta)]))
    return np.stack(tables).astype(np.float32).astype(ml_dtypes.bfloat16)


def x_tables():
    x, y, zl, i = np.meshgrid(np.arange(4), np.arange(4), np.arange(2), np.arange(8), indexing="ij")
    synth, fold = [], []
    for parity in range(2):
        kx = (x * 8 + zl * 4 + y) * 16 + 2 * i + parity
        theta = angles(kx.reshape(-1), np.arange(HALF), PX).reshape(4, 4, 2, 8, HALF)
        basis = np.stack([np.cos(theta), -np.sin(theta)], axis=2).astype(np.float32)
        weight = np.where(kx == 0, 1.0, 2.0).astype(np.float32)[:, :, None, :, :, None]
        synth.append((weight * basis).reshape(512, HALF).T)
        fold.append(basis.reshape(512, HALF))
    return (
        np.stack(synth).astype(ml_dtypes.bfloat16),
        np.stack(fold).astype(ml_dtypes.bfloat16),
    )


def mover(turned):
    row, column = (lax.broadcasted_iota(jnp.int32, (256, 256), axis) for axis in (turned, 1 - turned))
    kx = ((row & 7) << 1) | ((row >> 3) & 1)
    source = (kx << 4) | (((row >> 5) & 3) << 2) | ((row >> 7) << 1) | ((row >> 4) & 1)
    return (column == source).astype(jnp.float32).astype(BF)


def sorter(turned):
    row, column = (lax.broadcasted_iota(jnp.int32, (256, 256), axis) for axis in (turned, 1 - turned))
    return (row == (((column & 127) << 1) | (column >> 7))).astype(jnp.float32).astype(BF)


def wait(copies):
    for copy in copies:
        copy.wait()


def dot(a, b):
    return jnp.dot(a, b, preferred_element_type=jnp.float32)


def place_kernel(inv_ref, w_ref):
    row, column = (lax.broadcasted_iota(jnp.int32, (128, 128), axis) for axis in range(2))
    same = row % 4 == column % 4
    tall = (row[:, :32] // 4 == column[:, :32]).astype(BF)
    wide = (lax.broadcasted_iota(jnp.int32, (32, 128), 0) == lax.broadcasted_iota(jnp.int32, (32, 128), 1) // 4).astype(BF)
    for index in range(NCLASS):
        rows = dot(tall, inv_ref[index]).astype(BF)
        w_ref[:, index * 128 : index * 128 + 128] = jnp.where(same, dot(rows, wide), 0.0).astype(BF)


def pack_kernel(pos, v_hbm, *refs, half):
    own, outs, (v_ref, sems) = refs[:-6], refs[-6:-2], refs[-2:]
    copies = []
    for c in range(3):
        for z in range(4):
            first = pl.multiple_of(z * 32 + pos[3] * 16, 16)
            copies.append(pltpu.make_async_copy(v_hbm.at[c, :, pl.ds(first, 16)], v_ref.at[c, z], sems.at[c, z]))
            copies[-1].start()
    move, sort = mover(0), sorter(0)
    wait(copies)
    parts = []
    for step in range(4):
        z = lax.rem(pos[2] + step, 4)
        parts += [v_ref[c, z].reshape(256, 128) for c in range(3)]
    moved = dot(move, jnp.concatenate(parts, axis=1)).astype(BF)
    parts = []
    for i in range(12):
        part = moved[:, i * 128 : i * 128 + 128]
        parts.append(jnp.concatenate([part[:128], part[128:]], axis=1))
    moved = dot(jnp.concatenate(parts, axis=0), sort).astype(BF)
    for step in range(4):
        if half:
            outs[step][0] = own[step][0]
        outs[step][half] = moved[step * 384 : (step + 1) * 384].reshape(3, 4, 2, 16, 256)


def hold_kernel(*refs):
    pass


def preload_kernel(after_ref, inv_ref, *refs):
    copies = [pltpu.make_async_copy(refs[i], refs[3 + i], refs[7].at[i]) for i in range(3)]
    for copy in copies:
        copy.start()
    place_kernel(inv_ref, refs[6])
    wait(copies)


def gather_kernel(n_ref, out_ref):
    out_ref[...] = n_ref[:, 1]


def z_copies(table_hbm, table_ref, sems):
    return [pltpu.make_async_copy(table_hbm.at[p], table_ref.at[p], sems.at[p]) for p in range(2)]


def synth_kernel(pos, r0, e1, e2, e3, l1, l2, l3, table_ref, out_ref, lhs):
    nc = 3

    def fill(step, block):
        z = lax.rem(pos[2] + 4 - step, 4)
        for core in range(2):
            quarter = (z // 2) * 2 + lax.rem(pos[3] + core, 2)
            lanes = pl.ds(pl.multiple_of(quarter * 128, 128), 128)
            for ri in range(2):
                rows = pl.ds(pl.multiple_of(ri * (128 * nc) + lax.rem(z, 2) * (64 * nc), 64), 64 * nc)
                part = block[core, :, :, ri].reshape(64 * nc, 256)
                for parity in range(2):
                    lhs[parity, rows, lanes] = part[:, parity * 128 : parity * 128 + 128]

    fill(0, r0)

    @pl.when(pos[3] == EARLY)
    def _():
        for step, block in enumerate((e1, e2, e3)):
            fill(step + 1, block)

    @pl.when(pos[3] != EARLY)
    def _():
        for step, block in enumerate((l1, l2, l3)):
            fill(step + 1, block)

    n = 128 * nc
    sums = []
    for parity in range(2):
        by_cos = dot(lhs[parity], table_ref[parity, 0])
        by_sin = dot(lhs[parity], table_ref[parity, 1])
        sums.append((by_cos[:n] - by_sin[n:], by_sin[:n] + by_cos[n:]))
    for ri in range(2):
        even, odd = sums[0][ri], sums[1][ri]
        for half, both in enumerate((even + odd, even - odd)):
            part = both.reshape(2, nc, 4, 2, 8, HALF)
            for plane in range(4):
                for c in range(nc):
                    mixed = [part[zl, c, plane, parity] for parity in range(2) for zl in range(2)]
                    mixed = jnp.concatenate(mixed, axis=0).astype(BF)
                    for quarter in range(2):
                        out_ref[plane * 4 + half * 2 + quarter, c, ri] = mixed[:, quarter * 384 : quarter * 384 + 384]


def middle_kernel(d_ref, synth_ref, fold_ref, table_hbm, out_ref, table_ref, data, prod, sem, *, scale):
    table_copy = pltpu.make_async_copy(table_hbm, table_ref, sem)
    table_copy.start()
    for parity in range(2):
        for c in range(3):
            part = d_ref[:, c, :, parity * 16 : parity * 16 + 16, :].reshape(512, 384)
            data[parity, :, c * 384 : c * 384 + 384] = part
    for step in range(3):
        rows = slice(step * 256, step * 256 + 256)
        even = dot(synth_ref[0, rows, :], data[0])
        odd = dot(synth_ref[1, rows, :], data[1])
        low, high = even + odd, even - odd
        for c in range(3):
            lanes = slice(c * 384, c * 384 + 384)
            one, two = low[:, lanes] * low[:, 384:768], high[:, lanes] * high[:, 384:768]
            prod[0, rows, lanes] = (one + two).astype(BF)
            prod[1, rows, lanes] = (one - two).astype(BF)
    for parity in range(2):
        spectra = (dot(fold_ref[parity], prod[parity]) * scale).astype(BF)
        for c in range(3):
            part = spectra[:, c * 384 : c * 384 + 384].reshape(16, 2, 16, 384)
            out_ref[:, c, :, parity * 16 : parity * 16 + 16, :] = part
    table_copy.wait()


def analyse_kernel(pos, b_ref, table_ref, out_ref, lhs, *, scale):
    nc = 3
    n = 128 * nc
    for plane in range(4):
        for quarter in range(2):
            for ri in range(2):
                low = b_ref[plane * 4 + quarter, :, ri].reshape(32 * nc, 384).astype(jnp.float32)
                high = b_ref[plane * 4 + quarter + 2, :, ri].reshape(32 * nc, 384).astype(jnp.float32)
                rows = slice(ri * n + plane * 32 * nc, ri * n + plane * 32 * nc + 32 * nc)
                lanes = slice(quarter * 384, quarter * 384 + 384)
                lhs[0, rows, lanes] = (low + high).astype(BF)
                lhs[1, rows, lanes] = (low - high).astype(BF)
    for parity in range(2):
        by_cos, by_sin = (
            lax.dot_general(
                lhs[parity], table_ref[parity, i], (((1,), (1,)), ((), ())), preferred_element_type=jnp.float32
            )
            for i in range(2)
        )
        for ri, spectra in enumerate((by_cos[:n] + by_sin[n:], by_cos[n:] - by_sin[:n])):
            part = (spectra * scale).reshape(4, nc, 2, 2, 8, 512)
            for zl in range(2):
                for quarter in range(4):
                    for plane in range(4):
                        for c in range(nc):
                            piece = part[plane, c, :, zl, :, quarter * 128 : quarter * 128 + 128]
                            block, other = zl * 2 + quarter // 2, lax.rem(quarter + pos[3], 2)
                            lanes = slice(parity * 128, parity * 128 + 128)
                            out_ref[block, other, c, plane, ri, :, lanes] = piece.reshape(16, 128).astype(BF)


def right_rows(pos, count_ref, blocks, other, v_ref, store):
    move, sort = mover(1), sorter(1)
    row = lax.broadcasted_iota(jnp.int32, (16, 16, 128), 1)
    kx = lax.broadcasted_iota(jnp.int32, (16, 16, 128), 0)
    lane = lax.broadcasted_iota(jnp.int32, (16, 16, 128), 2)
    index = ((pos[2] // 2) * 2 + pos[3]) * 256 + lane + 128 * (lax.rem(row, 4) // 2)
    wavenumber = jnp.where(index < KZ // 2, index, index - KZ)
    counts = jnp.concatenate([jnp.full((1, 16, 128), count_ref[k], jnp.int32) for k in range(16)], axis=0)
    mean = (kx + pos[4] == 0) & (wavenumber == 0)
    half = jnp.where((jnp.abs(wavenumber) < counts) & jnp.logical_not(mean), 0.5, 0.0).astype(jnp.float32)
    both = dot(jnp.concatenate([block.reshape(128, 256) for block in blocks], axis=0), sort).astype(BF)
    both = [both[i * 128 : i * 128 + 128] for i in range(12)]
    both = [jnp.concatenate([part[:, :128], part[:, 128:]], axis=0) for part in both]
    moved = dot(move, jnp.concatenate(both, axis=1))
    for place in range(4):
        z = (place % 2) * 2 + place // 2
        rows = pl.ds(pl.multiple_of((z * 2 + lax.rem(pos[3] + other, 2)) * 16, 16), 16)
        for c in range(3):
            old = v_ref[c, :, rows, :].astype(jnp.float32)
            lanes = slice((place * 3 + c) * 128, (place * 3 + c) * 128 + 128)
            new = (old + moved[:, lanes].reshape(16, 16, 128) * half).astype(BF)
            for k in range(16):
                store(rows, place, c, k, new[k])


def right_kernel(pos, count_ref, n_ref, v_ref, out_ref):
    def store(rows, place, c, k, value):
        out_ref[k // 2, place, :, (c * 2 + k % 2) * 128 : (c * 2 + k % 2) * 128 + 128] = value

    right_rows(pos, count_ref, [n_ref[place, 0, c] for place in range(4) for c in range(3)], 0, v_ref, store)


def solve_kernel(pos, count_ref, right_ref, other_ref, v_ref, w_ref, class_ref, out_ref, right, done, sems):
    def store(rows, place, c, k, value):
        right[k // 2, rows, (c * 2 + k % 2) * 128 : (c * 2 + k % 2) * 128 + 128] = value

    right_rows(pos, count_ref, [other_ref[place, c] for place in range(4) for c in range(3)], 1, v_ref, store)
    for place in range(4):
        z = (place % 2) * 2 + place // 2
        rows = pl.ds(pl.multiple_of((z * 2 + pos[3]) * 16, 16), 16)
        for pair in range(8):
            right[pair, rows, :] = right_ref[pair, place]
    early = (lax.broadcasted_iota(jnp.int32, (16, 128), 0) & 3) < 2
    copies = []
    for pair in range(8):
        classes = []
        for k in range(2):
            line = class_ref[pair * 2 + k : pair * 2 + k + 1, :]
            classes.append(jnp.where(early, line[:, :128], line[:, 128:]))
        classes = jnp.concatenate(classes * 3, axis=1)
        line = right[pair].reshape(8, 16, 768)
        masked = []
        for index in range(NCLASS):
            chosen = (classes == index).astype(jnp.float32).astype(BF)
            masked.append((line * chosen[None]).reshape(128, 768))
        total = dot(w_ref[...], jnp.concatenate(masked, axis=0))
        block = pl.ds(pair * 2, 2)
        for c in range(3):
            for k in range(2):
                done[c, pair * 2 + k] = total[:, (c * 2 + k) * 128 : (c * 2 + k) * 128 + 128]
            copies.append(pltpu.make_async_copy(done.at[c, block], out_ref.at[c, block], sems.at[c, pair]))
            copies[-1].start()
    wait(copies)


def params():
    return pltpu.CompilerParams(vmem_limit_bytes=VMEM)


def in_hbm(array):
    return pltpu.with_memory_space_constraint(array, pltpu.HBM)


def spec(memory):
    return pl.BlockSpec(memory_space=memory)


def along_z(block, step, core):
    pairs = []
    for z in range(4):
        to = (z + step) % 4
        pairs.append((((z % 2) * 2 + z // 2) * 2 + core, ((to % 2) * 2 + to // 2) * 2 + core))
    return lax.ppermute(block, ("zl", "zh", "core"), pairs)


def plane(blocks):
    return lax.all_to_all(blocks, ("x", "y"), split_axis=0, concat_axis=0, tiled=True)


def after(value, *earlier):
    return lax.optimization_barrier((value, *earlier))[0]


def body(velocity, inverses, class_index, keep_count):
    scale_x = (0.5 / math.sqrt(KX * KZ)) ** 2 / PX
    scale_z = 2.0 * math.sqrt(KX * KZ) / PZ
    z_basis, x_synth, x_fold = (in_hbm(jnp.asarray(t)) for t in (z_tables(), *x_tables()))
    z_scratch = [pltpu.VMEM((2, 2, 512, HALF), BF), pltpu.SemaphoreType.DMA((2,))]
    lines = velocity.reshape(3, 16, NY, 2, 2, 128).transpose(0, 1, 2, 4, 3, 5).reshape(3, 16, 128, 128)
    x, y, zl = (lax.axis_index(name) for name in ("x", "y", "zl"))
    pos = jnp.stack([x, y, lax.axis_index("zh") * 2 + zl, lax.axis_index("core"), (x * 8 + zl * 4 + y) * 16])

    mode_shape = jax.ShapeDtypeStruct((2, 3, 4, 2, 16, 256), BF)
    plane_shape = jax.ShapeDtypeStruct((16, 3, 2, 32, 384), BF)
    table_shape = pltpu.VMEM((2, 2, 512, HALF), BF)
    smem, vmem, hbm, free = (spec(m) for m in (pltpu.SMEM, pltpu.VMEM, pltpu.HBM, pl.ANY))

    def call(kernel, name, specs, args, outs, scratch, aliases={}, out_spec=vmem):
        return pl.pallas_call(
            kernel,
            in_specs=specs,
            out_specs=[out_spec] * len(outs),
            out_shape=outs,
            scratch_shapes=scratch,
            input_output_aliases=aliases,
            compiler_params=params(),
            name=name,
        )(*args)

    half_shape = jax.ShapeDtypeStruct((1, 3, 4, 2, 16, 256), BF)
    dma = pltpu.SemaphoreType.DMA
    fixed = in_hbm(lines)
    other = lax.ppermute(velocity, "core", [(0, 1), (1, 0)])
    other = other.reshape(3, 16, NY, 2, 2, 128).transpose(0, 1, 2, 4, 3, 5).reshape(3, 16, 128, 128)
    scratch = [pltpu.VMEM((3, 4, 16, 16, 128), BF), dma((3, 4))]
    packed = call(
        functools.partial(pack_kernel, half=0), "pack", [smem, hbm], (pos, fixed), [half_shape] * 4, scratch
    )
    packed = call(
        functools.partial(pack_kernel, half=1), "pack", [smem, free] + [vmem] * 4, (pos, other, *packed),
        [mode_shape] * 4, scratch,
    )
    first = [along_z(packed[step], step, EARLY) for step in (1, 2, 3)]
    table, *x_held, operators = call(
        preload_kernel, "preload", [free, vmem] + [hbm] * 3, (packed[0], inverses, z_basis, x_synth, x_fold),
        [
            table_shape, pltpu.VMEM((2, HALF, 512), BF), pltpu.VMEM((2, 512, HALF), BF),
            jax.ShapeDtypeStruct((128, NCLASS * 128), BF),
        ],
        [dma((3,))],
    )
    token = packed[0][0, 0, 0, 0, :, :128]
    token = lax.ppermute(token, "core", [(EARLY, 1 - EARLY)])
    held = call(
        hold_kernel, "hold", [free] * 5, (token, table, packed[1], packed[2], packed[3]), [mode_shape] * 3, [],
        {2: 0, 3: 1, 4: 2}, free,
    )
    ready = {1: held[0], 2: held[1], 3: held[2]}
    second = [along_z(ready[step], step, 1 - EARLY) for step in (1, 2, 3)]
    (spread,) = call(
        synth_kernel, "synth", [smem] + [vmem] * 8, (pos, packed[0], *first, *second, table), [plane_shape],
        [pltpu.VMEM((2, 768, 512), BF)],
    )
    folded, table = call(
        functools.partial(middle_kernel, scale=scale_x), "middle", [vmem] * 3 + [hbm],
        (plane(spread), *x_held, z_basis), [plane_shape, table_shape],
        [
            pltpu.VMEM((2, 512, 1152), BF), pltpu.VMEM((2, HALF, 1152), BF), dma(()),
        ],
    )
    (modes,) = call(
        functools.partial(analyse_kernel, scale=scale_z), "analyse", [smem, vmem, vmem],
        (pos, plane(folded), table), [jax.ShapeDtypeStruct((4, *mode_shape.shape), BF)],
        [pltpu.VMEM((2, 768, HALF), BF)],
    )
    modes = lax.all_to_all(modes, COLUMN, split_axis=0, concat_axis=0, tiled=True)
    (other,) = call(gather_kernel, "gather", [vmem], (modes,), [jax.ShapeDtypeStruct((4, 3, 4, 2, 16, 256), BF)], [])
    other = lax.ppermute(other, "core", [(0, 1), (1, 0)])
    (right,) = call(
        right_kernel, "right", [smem] * 2 + [vmem] * 2, (pos, keep_count, modes, lines),
        [jax.ShapeDtypeStruct((8, 4, 16, 768), BF)], [],
    )
    (solved,) = call(
        solve_kernel, "solve", [smem] * 2 + [vmem] * 5,
        (pos, keep_count, right, other, lines, operators, class_index),
        [jax.ShapeDtypeStruct((3, 16, 128, 128), jnp.float32)],
        [pltpu.VMEM((8, 128, 768), BF), pltpu.VMEM((3, 16, 128, 128), jnp.float32), dma((3, 8))],
        out_spec=free,
    )
    return solved.reshape(3, 16, NY, 2, 2, 128).transpose(0, 1, 2, 4, 3, 5).reshape(3, 16, NY, 2, 256)


def solution(mesh):
    fine = Mesh(mesh.devices.reshape(4, 2, 4, 2, 2), ("x", "zl", "y", "zh", "core"))
    wide, narrow = ("x", "zl", "y"), ("zh", "core")
    in_specs = (P(None, wide, None, None, narrow), P(), P(wide, narrow), P(wide))
    out_specs = P(None, wide, None, None, narrow)
    return jax.shard_map(body, mesh=fine, in_specs=in_specs, out_specs=out_specs, check_vma=False)
```
